128 devices in a mesh: row: 8 (over z_hi, x), col: 16 (over y, z_lo, core).
Axes of the slice: x: 4, y: 4, z: 4 (z_hi: 2, z_lo: 2; z = z_hi * 2 + z_lo), core: 2. Of those that a mesh axis runs over, the one named last changes fastest.
Arguments:
- view_one: bfloat16 [1024, 16384], P(('row', 'col')), may hold values from -70 to 70
- view_two: bfloat16 [1024, 16384], P(('row', 'col')), may hold values from -70 to 70
Outputs:
- grad_one: float32 [1024, 16384], P(('row', 'col'))
- grad_two: float32 [1024, 16384], P(('row', 'col'))
- total_loss: float32 [], replicated
The draws below stay inside these ranges and needn't reach their ends.
All inputs are finite; a program needn't handle non-finite values.
Results may differ from the reference program's by a relative error of at most 0.0031.
Values may be sent and summed in bfloat16 or wider, within the bound.
No kernel may reach another device: no remote copies, remote signals or barrier semaphores. Data moves between devices by JAX's collectives and lax.ppermute only.
A program may use at most 128 MiB of HBM per device.

```python
import math
import jax
import jax.numpy as jnp
from jax import lax

F = 16384
N = 1024


def shared_parts(key):
    keys = jax.random.split(key, 4)
    gauss = jnp.clip(jax.random.normal(keys[0], (N, F), jnp.float32), -4.0, 4.0)
    base = gauss
    col_log = jax.random.uniform(keys[2], (1, F), jnp.float32, -1.2, 1.2)
    row_log = jax.random.uniform(keys[3], (N, 1), jnp.float32, -0.7, 0.7)
    trend = 0.6 + 0.8 * jnp.arange(F, dtype=jnp.float32)[None, :] / F
    return (base, jnp.exp(col_log + row_log) * trend)


def draw_view_one(key, part):
    base, scales = shared_parts(key)
    key = jax.random.fold_in(key, 11)
    noise = jnp.clip(jax.random.normal(key, (N, F), jnp.float32), -4.0, 4.0)
    return (scales * (base + 0.6 * noise)).astype(jnp.bfloat16)


def draw_view_two(key, part):
    base, scales = shared_parts(key)
    key = jax.random.fold_in(key, 12)
    noise = jnp.clip(jax.random.normal(key, (N, F), jnp.float32), -4.0, 4.0)
    return (scales * (base + 0.6 * noise)).astype(jnp.bfloat16)


def setup_inputs(seed: int = 0) -> dict:
    key_of = jax.random.split(jax.random.key(seed), 3)
    view_one = draw_view_one(jax.random.fold_in(key_of[2], 71), 0)
    view_two = draw_view_two(jax.random.fold_in(key_of[2], 71), 0)
    return dict(view_one=view_one, view_two=view_two)


epsilon = 0.0001
inv_weight = 25.0
var_weight = 25.0
cov_weight = 1.0
out_scale = 25.0

def center(view):
    values = view.astype(jnp.float32)
    col_total = lax.optimization_barrier(jnp.sum(values, axis=0)) / N
    centered = values - col_total
    spread = jnp.sqrt(lax.optimization_barrier(jnp.sum(centered * centered, axis=0)) / (N - 1) + epsilon)
    return (centered, spread)

def view_terms(view):
    centered, spread = center(view)
    rounded = centered.astype(jnp.bfloat16).astype(jnp.float32)
    block_width = math.gcd(F, 1024)
    feature_ids = jnp.arange(F, dtype=jnp.int32)[:, None]

    def scan_step(state_pair, offset):
        total_grad, cov_sum = state_pair
        first_col = (offset * block_width).astype(jnp.int32)
        columns = lax.dynamic_slice_in_dim(rounded, first_col, block_width, 1)
        cov_tile = lax.dot_general(rounded, columns, (((0,), (0,)), ((), ())), precision=lax.Precision.HIGHEST, preferred_element_type=jnp.float32) / (N - 1)
        on_diagonal = feature_ids == first_col + jnp.arange(block_width, dtype=jnp.int32)[None, :]
        off_diag = jnp.where(on_diagonal, 0.0, cov_tile)
        cov_sum = cov_sum + jnp.sum(off_diag * off_diag)
        tile_round = off_diag.astype(jnp.bfloat16).astype(jnp.float32)
        total_grad = total_grad + lax.dot_general(columns, tile_round, (((1,), (1,)), ((), ())), precision=lax.Precision.HIGHEST, preferred_element_type=jnp.float32)
        return ((total_grad, cov_sum), None)
    start_state = (jnp.zeros((N, F), jnp.float32), jnp.zeros((), jnp.float32))
    final_state, unused = lax.scan(scan_step, start_state, jnp.arange(F // block_width, dtype=jnp.int32))
    total_grad, cov_sum = final_state
    hinge_sum = jnp.sum(jnp.maximum(1.0 - spread, 0.0))
    feat_grad = 4.0 * cov_weight * N / (N - 1) * total_grad - var_weight * N / (N - 1) * jnp.where(spread < 1.0, centered / spread, 0.0)
    return (feat_grad, cov_sum, hinge_sum)

def reference(view_one, view_two):
    grad_first, cov_first, hinge_first = view_terms(view_one)
    grad_second, cov_second, hinge_second = view_terms(view_two)
    view_diff = view_one.astype(jnp.float32) - view_two.astype(jnp.float32)
    total_loss = inv_weight * jnp.sum(view_diff * view_diff) / (N * F) + var_weight * (hinge_first + hinge_second) / F + cov_weight * (cov_first + cov_second) / F
    grad_one = (grad_first + 2.0 * inv_weight * view_diff) / out_scale
    grad_two = (grad_second - 2.0 * inv_weight * view_diff) / out_scale
    return (grad_one, grad_two, total_loss)
```

```python
import jax
import jax.numpy as jnp
import numpy as np
from jax import lax
from jax.sharding import Mesh
from jax.sharding import PartitionSpec as P

epsilon = 0.0001
inv_weight = 25.0
var_weight = 25.0
cov_weight = 1.0
out_scale = 25.0

FINE = ("zh", "x", "y", "zl", "core")
SIZES = (2, 4, 4, 2, 2)
ROW_GROUP = ("x", "core")
FEATURE_GROUP = ("zh", "y", "zl")
SWAP = ((0, 1), (1, 0))
NEAR = ((0, 1), (1, 0), (2, 3), (3, 2))
FAR = ((0, 2), (2, 0), (1, 3), (3, 1))


def to_bf16(values):
    return lax.reduce_precision(values, 8, 7)


def gram_part(halves, first_row, group_rows, batch_rows):
    product = 0.0
    stats = []
    for raw in halves:
        values = raw.astype(jnp.float32)
        centered = values - jnp.sum(values, axis=0) / batch_rows
        spread = jnp.sqrt(jnp.sum(centered * centered, axis=0) / (batch_rows - 1) + epsilon)
        wide = to_bf16(centered)
        rounded = wide.astype(jnp.bfloat16)
        energy = jnp.sum(wide * wide, axis=0)
        mine = lax.dynamic_slice_in_dim(rounded, first_row, group_rows, 0)
        product = product + lax.dot_general(
            mine, rounded, (((1,), (1,)), ((), ())), preferred_element_type=jnp.float32
        )
        hinge = jnp.where(
            spread < 1.0,
            lax.dynamic_slice_in_dim(centered, first_row, group_rows, 0) / spread,
            0.0,
        )
        stats.append((rounded, mine, energy, spread, hinge))
    return product, stats


def body(view_one, view_two):
    shard_rows, feature_count = view_one.shape
    x_size, core_size = lax.axis_size("x"), lax.axis_size("core")
    feature_parts = lax.axis_size("zh") * lax.axis_size("y") * lax.axis_size("zl")
    row_parts = x_size * core_size
    device_count = row_parts * feature_parts
    batch_rows = shard_rows * device_count
    group_rows = batch_rows // row_parts
    half_width = feature_count // feature_parts // core_size
    core = lax.axis_index("core")
    first_row = (lax.axis_index("x") * core_size + core) * group_rows
    views = jnp.stack([view_one, view_two])

    blocks = views.reshape(2, shard_rows, feature_parts, core_size, half_width)
    blocks = blocks.transpose(3, 2, 0, 1, 4)
    blocks = jnp.broadcast_to(blocks[None], (x_size,) + blocks.shape)
    blocks = blocks.reshape(device_count, 2, shard_rows, half_width)
    own = lax.all_to_all(blocks, ROW_GROUP + FEATURE_GROUP, 0, 0, tiled=True)
    other = lax.ppermute(own, "core", SWAP)

    parts, stats, scalar = [], [], 0.0
    for v in range(2):
        halves = [a[:, v].reshape(batch_rows, half_width) for a in (own, other)]
        product, stat = gram_part(halves, first_row, group_rows, batch_rows)
        parts.append(product.astype(jnp.bfloat16).reshape(feature_parts, shard_rows, batch_rows))
        stats.append(stat)
        scalar += var_weight / feature_count * sum(
            jnp.sum(jnp.maximum(1.0 - s[3], 0.0)) for s in stat
        ) / row_parts
        scalar -= cov_weight / feature_count / (batch_rows - 1) ** 2 * sum(
            jnp.sum(s[2] * s[2]) for s in stat
        ) / row_parts

    pieces = lax.all_to_all(jnp.stack(parts, 1), FEATURE_GROUP, 0, 0, tiled=True)
    pieces = jnp.sum(pieces.astype(jnp.float32), axis=0)
    scalar += cov_weight / feature_count / (batch_rows - 1) ** 2 * jnp.sum(pieces * pieces)
    view_diff = view_one.astype(jnp.float32) - view_two.astype(jnp.float32)
    scalar += inv_weight / (batch_rows * feature_count) * jnp.sum(view_diff * view_diff)

    ids = lax.broadcasted_iota(jnp.int32, (shard_rows, batch_rows), 1)
    row_ids = lax.broadcasted_iota(jnp.int32, (shard_rows, batch_rows), 0)
    feature_idx = lax.axis_index(FEATURE_GROUP)
    on_diagonal = ids == first_row + feature_idx * shard_rows + row_ids
    sent = to_bf16(pieces)
    lost = jnp.sum(jnp.where(on_diagonal, pieces - sent, 0.0), axis=2, keepdims=True)
    high = to_bf16(scalar)
    middle = to_bf16(scalar - high)
    low = scalar - high - middle
    lanes = lax.broadcasted_iota(jnp.int32, (2, shard_rows, 128), 2)
    extra = jnp.where(lanes == 0, lost, 0.0)
    for lane, value in ((1, high), (2, middle), (3, low)):
        extra = jnp.where(lanes == lane, value, extra)
    sent = jnp.concatenate([sent, extra], axis=2).astype(jnp.bfloat16)
    gram = jnp.broadcast_to(sent[None], (feature_parts,) + sent.shape)
    gram = lax.all_to_all(gram, FEATURE_GROUP, 0, 0, tiled=True)
    total_loss = jnp.sum(gram[:, 0, 0, batch_rows + 1 : batch_rows + 4].astype(jnp.float32))
    for axis, pairs in (("core", SWAP), ("x", NEAR), ("x", FAR)):
        total_loss = total_loss + lax.ppermute(total_loss, axis, pairs)

    factor_cov = 4.0 * cov_weight * batch_rows / (batch_rows - 1)
    factor_var = var_weight * batch_rows / (batch_rows - 1)
    grads = []
    for v in range(2):
        rows = gram[:, v, :, :batch_rows].reshape(group_rows, batch_rows)
        lost = gram[:, v, :, batch_rows].reshape(group_rows, 1).astype(jnp.float32)
        for rounded, mine, energy, spread, hinge in stats[v]:
            product = lax.dot_general(
                rows, rounded, (((1,), (0,)), ((), ())), preferred_element_type=jnp.float32
            )
            product = (product - mine.astype(jnp.float32) * (energy - lost)) / (batch_rows - 1)
            grad = (factor_cov * product - factor_var * hinge) / out_scale
            grads.append(grad.astype(jnp.bfloat16).reshape(feature_parts, shard_rows, half_width))
    grads = jnp.stack(grads, 1)
    grads = lax.all_to_all(grads, FEATURE_GROUP, 0, 0, tiled=True)
    grads = grads.reshape(feature_parts, 2, core_size, shard_rows, half_width).astype(jnp.float32)
    grads = jnp.where(core == 0, grads, grads[:, :, ::-1])
    grads = grads.transpose(1, 3, 0, 2, 4).reshape(2, shard_rows, feature_count)
    push = 2.0 * inv_weight / out_scale * view_diff
    return grads[0] + push, grads[1] - push, total_loss


def solution(mesh):
    fine = Mesh(np.asarray(mesh.devices).reshape(SIZES), FINE)
    rows = P(FINE, None)
    return jax.shard_map(
        body, mesh=fine, in_specs=(rows, rows), out_specs=(rows, rows, P()), check_vma=False
    )
```

```python
import functools

import jax
import jax.numpy as jnp
import numpy as np
from jax import lax
from jax.experimental import pallas as pl
from jax.experimental.pallas import tpu as pltpu
from jax.sharding import Mesh
from jax.sharding import PartitionSpec as P

epsilon = 0.0001
inv_weight = 25.0
var_weight = 25.0
cov_weight = 1.0
out_scale = 25.0

FINE = ("zh", "x", "y", "zl", "core")
SIZES = (2, 4, 4, 2, 2)
FEATURE_GROUP = ("zh", "y", "zl")
CHIPS = ("x",) + FEATURE_GROUP
SWAP = ((0, 1), (1, 0))
NEAR = ((0, 1), (1, 0), (2, 3), (3, 2))
FAR = ((0, 2), (2, 0), (1, 3), (3, 1))
LANES = 128
VMEM_BYTES = 48 * 1024 * 1024
CONTRACT_LAST = (((1,), (1,)), ((), ()))
CONTRACT_FIRST = (((1,), (0,)), ((), ()))


def of_view(block, v):
    devices, rows, width = block.shape
    half = rows // 2
    return block[:, v * half : (v + 1) * half].reshape(devices * half, width)


def both_views(first, second, devices):
    shape = (devices, first.shape[0] // devices, first.shape[1])
    return jnp.concatenate([first.reshape(shape), second.reshape(shape)], axis=1)


def gram_kernel(sizes, place, own, other, rounded, part, rest, share, total):
    batch_rows, feature_count, feature_parts, row_parts = sizes
    group_rows = batch_rows // row_parts
    step = pl.program_id(0)
    first_row = pl.multiple_of(place[0] * group_rows, group_rows)
    first_device = place[0] * feature_parts
    factor_cov = 4.0 * cov_weight * batch_rows / (batch_rows - 1) ** 2 / out_scale
    factor_var = var_weight * batch_rows / (batch_rows - 1) / out_scale
    half = batch_rows // 2
    shares = 0.0
    products = []
    for v in range(2):
        a = of_view(own[...].astype(jnp.float32), v)
        b = of_view(other[...].astype(jnp.float32), v)
        mean = (jnp.sum(a, axis=0, keepdims=True) + jnp.sum(b, axis=0, keepdims=True)) / batch_rows
        a = a - mean
        b = b - mean
        square = jnp.sum(a * a, axis=0, keepdims=True) + jnp.sum(b * b, axis=0, keepdims=True)
        spread = jnp.sqrt(square / (batch_rows - 1) + epsilon)
        a = a.astype(jnp.bfloat16)
        b = b.astype(jnp.bfloat16)
        rounded[v, :half] = a
        rounded[v, half:] = b
        a = a.astype(jnp.float32)
        b = b.astype(jnp.float32)
        energy = jnp.sum(a * a, axis=0, keepdims=True) + jnp.sum(b * b, axis=0, keepdims=True)
        mine = rounded[v, pl.ds(first_row, group_rows)]
        products.append(
            lax.dot_general(mine, rounded[v], CONTRACT_LAST, preferred_element_type=jnp.float32)
        )
        centered = of_view(own[pl.ds(first_device, feature_parts)].astype(jnp.float32), v) - mean
        hinge = jnp.where(spread < 1.0, centered / spread, 0.0)
        rest[v] = -factor_var * hinge - factor_cov * (mine.astype(jnp.float32) * energy)
        shares += var_weight / feature_count / row_parts * jnp.maximum(1.0 - spread, 0.0)
        shares -= cov_weight / feature_count / row_parts * (energy / (batch_rows - 1)) ** 2
    share[...] = shares

    @pl.when(step == 0)
    def _():
        for v in range(2):
            total[v] = products[v]

    @pl.when(step > 0)
    def _():
        for v in range(2):
            total[v] += products[v]

    @pl.when(step == pl.num_programs(0) - 1)
    def _():
        part[...] = both_views(total[0], total[1], feature_parts).astype(jnp.bfloat16)


def sum_kernel(sizes, place, inv, pieces, share, sent, scalar):
    batch_rows, feature_count, feature_parts, row_parts = sizes
    rows = pieces.shape[1] // 2
    summed = jnp.sum(pieces[...].astype(jnp.float32), axis=0)
    shape = summed.shape
    lane = lax.broadcasted_iota(jnp.int32, shape, 1)
    row = lax.broadcasted_iota(jnp.int32, shape, 0)
    diagonal = (place[0] * feature_parts + place[1]) * rows + row % rows
    short = summed.astype(jnp.bfloat16).astype(jnp.float32)
    lost = jnp.sum(jnp.where(lane == diagonal, summed - short, 0.0), axis=1, keepdims=True)
    extra = jnp.broadcast_to(lost, (shape[0], LANES))
    out = jnp.concatenate([short, extra], axis=1).astype(jnp.bfloat16)
    sent[...] = jnp.broadcast_to(out[None], sent.shape)
    factor = cov_weight / feature_count / (batch_rows - 1) ** 2
    value = factor * jnp.sum(summed * summed) + jnp.sum(share[...]) + inv[0]
    scalar[...] = jnp.full(scalar.shape, value, jnp.float32)


def grad_kernel(sizes, place, scalar, gram, rounded, rest, sent, whole):
    batch_rows, feature_count, feature_parts, row_parts = sizes
    group_rows = batch_rows // row_parts
    step = pl.program_id(0)
    width = rounded.shape[2]
    factor_cov = 4.0 * cov_weight * batch_rows / (batch_rows - 1) ** 2 / out_scale
    first_row = pl.multiple_of(place[0] * group_rows, group_rows)
    wide = gram[...].astype(jnp.float32)
    grads = []
    for v in range(2):
        rows = of_view(wide, v)
        lost = rows[:, batch_rows : batch_rows + 1]
        rows = rows[:, :batch_rows].astype(jnp.bfloat16)
        product = lax.dot_general(
            rows, rounded[v], CONTRACT_FIRST, preferred_element_type=jnp.float32
        )
        mine = rounded[v, pl.ds(first_row, group_rows)].astype(jnp.float32)
        grads.append(factor_cov * (product + lost * mine) + rest[v])
    place_out = pl.multiple_of(step * width, width)
    block = both_views(grads[0], grads[1], feature_parts).astype(jnp.bfloat16)
    sent[:, :, pl.ds(place_out, width)] = block

    @pl.when(step == 0)
    def _():
        shape = (whole.shape[1], LANES)
        value = jnp.full(shape, scalar[0], jnp.float32)
        high = value.astype(jnp.bfloat16).astype(jnp.float32)
        middle = (value - high).astype(jnp.bfloat16).astype(jnp.float32)
        low = value - high - middle
        lane = lax.broadcasted_iota(jnp.int32, shape, 1)
        parts = jnp.where(lane == 0, high, jnp.where(lane == 1, middle, low)).astype(jnp.bfloat16)
        whole[...] = jnp.broadcast_to(parts[None], whole.shape)


def body(view_one, view_two):
    shard_rows, feature_count = view_one.shape
    x_size, core_size = lax.axis_size("x"), lax.axis_size("core")
    feature_parts = lax.axis_size("zh") * lax.axis_size("y") * lax.axis_size("zl")
    row_parts = x_size * core_size
    chips = x_size * feature_parts
    batch_rows = shard_rows * row_parts * feature_parts
    group_rows = batch_rows // row_parts
    width = feature_count // feature_parts
    steps = 4
    chunk = width // steps
    sizes = (batch_rows, feature_count, feature_parts, row_parts)
    place = jnp.stack([lax.axis_index("x"), lax.axis_index(FEATURE_GROUP)]).astype(jnp.int32)
    params = pltpu.CompilerParams(vmem_limit_bytes=VMEM_BYTES)
    both = 2 * shard_rows

    blocks = jnp.concatenate([view_one, view_two]).reshape(both, feature_parts, width)
    blocks = blocks.transpose(1, 0, 2)
    blocks = jnp.broadcast_to(blocks[None], (x_size,) + blocks.shape).reshape(chips, both, width)
    own = lax.all_to_all(blocks, CHIPS, 0, 0, tiled=True)
    other = lax.ppermute(own, "core", SWAP)
    view_diff = view_one.astype(jnp.float32) - view_two.astype(jnp.float32)
    inv = inv_weight / (batch_rows * feature_count) * jnp.sum(view_diff * view_diff)

    rounded, part, rest, share = pl.pallas_call(
        functools.partial(gram_kernel, sizes),
        grid_spec=pltpu.PrefetchScalarGridSpec(
            num_scalar_prefetch=1,
            grid=(steps,),
            in_specs=[
                pl.BlockSpec((chips, both, chunk), lambda f, place: (0, 0, f)),
                pl.BlockSpec((chips, both, chunk), lambda f, place: (0, 0, f)),
            ],
            out_specs=[
                pl.BlockSpec((2, batch_rows, chunk), lambda f, place: (0, 0, f)),
                pl.BlockSpec((feature_parts, both, batch_rows), lambda f, place: (0, 0, 0)),
                pl.BlockSpec((2, group_rows, chunk), lambda f, place: (0, 0, f)),
                pl.BlockSpec((1, chunk), lambda f, place: (0, f)),
            ],
            scratch_shapes=[pltpu.VMEM((2, group_rows, batch_rows), jnp.float32)],
        ),
        out_shape=[
            jax.ShapeDtypeStruct((2, batch_rows, width), jnp.bfloat16),
            jax.ShapeDtypeStruct((feature_parts, both, batch_rows), jnp.bfloat16),
            jax.ShapeDtypeStruct((2, group_rows, width), jnp.float32),
            jax.ShapeDtypeStruct((1, width), jnp.float32),
        ],
        compiler_params=params,
        name="gram_part",
    )(place, own, other)

    pieces = lax.all_to_all(part, FEATURE_GROUP, 0, 0, tiled=True)
    smem = pl.BlockSpec(memory_space=pltpu.SMEM)
    vmem = pl.BlockSpec(memory_space=pltpu.VMEM)
    sent, scalar = pl.pallas_call(
        functools.partial(sum_kernel, sizes),
        in_specs=[smem, smem, vmem, vmem],
        out_specs=[vmem, vmem],
        out_shape=[
            jax.ShapeDtypeStruct((feature_parts, both, batch_rows + LANES), jnp.bfloat16),
            jax.ShapeDtypeStruct((8, LANES), jnp.float32),
        ],
        compiler_params=params,
        name="gram_sum",
    )(place, inv.reshape(1), pieces, share)

    gram = lax.all_to_all(sent, FEATURE_GROUP, 0, 0, tiled=True)
    for axis, pairs in (("core", SWAP), ("x", NEAR), ("x", FAR)):
        scalar = scalar + lax.ppermute(scalar, axis, pairs)

    grads, whole = pl.pallas_call(
        functools.partial(grad_kernel, sizes),
        grid_spec=pltpu.PrefetchScalarGridSpec(
            num_scalar_prefetch=2,
            grid=(steps,),
            in_specs=[
                pl.BlockSpec(sent.shape, lambda f, place, scalar: (0, 0, 0)),
                pl.BlockSpec((2, batch_rows, chunk), lambda f, place, scalar: (0, 0, f)),
                pl.BlockSpec((2, group_rows, chunk), lambda f, place, scalar: (0, 0, f)),
            ],
            out_specs=[
                pl.BlockSpec((feature_parts, both, width), lambda f, place, scalar: (0, 0, 0)),
                pl.BlockSpec((feature_parts, both, LANES), lambda f, place, scalar: (0, 0, 0)),
            ],
        ),
        out_shape=[
            jax.ShapeDtypeStruct((feature_parts, both, width), jnp.bfloat16),
            jax.ShapeDtypeStruct((feature_parts, both, LANES), jnp.bfloat16),
        ],
        compiler_params=params,
        name="grad_rows",
    )(place, scalar[0, :1], gram, rounded, rest)

    grads = jnp.concatenate([grads, whole], axis=2)
    grads = lax.all_to_all(grads, FEATURE_GROUP, 0, 0, tiled=True)
    total_loss = jnp.sum(grads[:, 0, width : width + 3].astype(jnp.float32))
    grads = grads[:, :, :width].reshape(feature_parts, 2, shard_rows, width).astype(jnp.float32)
    grads = grads.transpose(1, 2, 0, 3).reshape(2, shard_rows, feature_count)
    push = 2.0 * inv_weight / out_scale * view_diff
    return grads[0] + push, grads[1] - push, total_loss


def solution(mesh):
    fine = Mesh(np.asarray(mesh.devices).reshape(SIZES), FINE)
    rows = P(FINE, None)
    return jax.shard_map(
        body, mesh=fine, in_specs=(rows, rows), out_specs=(rows, rows, P()), check_vma=False
    )
```

```python
import functools

import jax
import jax.numpy as jnp
import numpy as np
from jax import lax
from jax.experimental import pallas as pl
from jax.experimental.pallas import tpu as pltpu
from jax.sharding import Mesh
from jax.sharding import PartitionSpec as P

epsilon = 0.0001
inv_weight = 25.0
var_weight = 25.0
cov_weight = 1.0
out_scale = 25.0

FINE = ("zh", "x", "y", "zl", "core")
SIZES = (2, 4, 4, 2, 2)
LANES = 128
VMEM_BYTES = 48 * 1024 * 1024
CONTRACT_LAST = (((1,), (1,)), ((), ()))
CONTRACT_FIRST = (((1,), (0,)), ((), ()))

IDS = np.arange(128).reshape(SIZES)
BY_RING = np.stack(
    [
        IDS[..., 0].transpose(1, 0, 2, 3).reshape(4, 16),
        IDS[..., 1].transpose(2, 0, 1, 3).reshape(4, 16),
    ]
)
GROUPS = [[int(i) for i in g] for core in BY_RING for g in core]
SWAP = [(int(i), int(i) ^ 1) for i in IDS.reshape(-1)]


def along_ring(source):
    return [
        (int(BY_RING[k, source[i], c]), int(BY_RING[k, i, c]))
        for k in range(2)
        for i in range(4)
        for c in range(16)
    ]


UP = along_ring((3, 0, 1, 2))
DOWN = along_ring((1, 2, 3, 0))
NEAR = along_ring((1, 0, 3, 2))
FAR = along_ring((2, 3, 0, 1))


def exchange(blocks):
    return lax.all_to_all(blocks, FINE, 0, 0, tiled=True, axis_index_groups=GROUPS)


def move(block, pairs):
    return lax.ppermute(block, FINE, pairs)


def pick(core, first, second):
    return jnp.where(core == 0, first, second)


def pack_kernel(core, view_one, view_two, got, packed):
    parts, rows, width = packed.shape
    for c in range(parts):
        cut = pl.ds(c * width, width)
        keep = pick(
            core[0], view_one[:, cut].astype(jnp.float32), view_two[:, cut].astype(jnp.float32)
        )
        both = jnp.concatenate([keep, got[:, cut].astype(jnp.float32)], axis=0)
        packed[c] = both.astype(jnp.bfloat16)


def gram_kernel(sizes, own, up, down, far_up, far_down, rounded, part, rest, share, total):
    batch_rows, feature_count, row_parts = sizes
    group_rows = batch_rows // row_parts
    step = pl.program_id(0)
    width = own.shape[2]
    factor_cov = 4.0 * cov_weight * batch_rows / (batch_rows - 1) ** 2 / out_scale
    factor_var = var_weight * batch_rows / (batch_rows - 1) / out_scale
    values = [
        ref[...].reshape(-1, width).astype(jnp.float32)
        for ref in (own, up, down, far_up, far_down)
    ]
    mean = sum(jnp.sum(a, axis=0, keepdims=True) for a in values) / batch_rows
    values = [a - mean for a in values]
    square = sum(jnp.sum(a * a, axis=0, keepdims=True) for a in values)
    spread = jnp.sqrt(square / (batch_rows - 1) + epsilon)
    energy = 0.0
    row = 0
    for a in values:
        a = a.astype(jnp.bfloat16)
        rounded[pl.ds(row, a.shape[0])] = a
        row += a.shape[0]
        a = a.astype(jnp.float32)
        energy += jnp.sum(a * a, axis=0, keepdims=True)
    mine = rounded[pl.ds(0, group_rows)]
    product = lax.dot_general(
        mine, rounded[...], CONTRACT_LAST, preferred_element_type=jnp.float32
    )
    hinge = values[0] * jnp.where(spread < 1.0, 1.0 / spread, 0.0)
    rest[...] = -factor_var * hinge - mine.astype(jnp.float32) * (factor_cov * energy)
    shares = var_weight / feature_count / row_parts * jnp.maximum(1.0 - spread, 0.0)
    share[...] = shares - cov_weight / feature_count / row_parts * (energy / (batch_rows - 1)) ** 2

    @pl.when(step == 0)
    def _():
        total[...] = product

    @pl.when(step > 0)
    def _():
        total[...] += product

    @pl.when(step == pl.num_programs(0) - 1)
    def _():
        part[...] = total[...].astype(jnp.bfloat16).reshape(part.shape)


def sum_kernel(sizes, place, inv, pieces, share, sent, scalar):
    batch_rows, feature_count, row_parts = sizes
    rows = pieces.shape[1]
    summed = jnp.sum(pieces[...].astype(jnp.float32), axis=0)
    shape = summed.shape
    lane = lax.broadcasted_iota(jnp.int32, shape, 1)
    row = lax.broadcasted_iota(jnp.int32, shape, 0)
    short = summed.astype(jnp.bfloat16).astype(jnp.float32)
    on_diagonal = lane == place[0] * rows + row
    lost = jnp.sum(jnp.where(on_diagonal, summed - short, 0.0), axis=1, keepdims=True)
    extra = jnp.broadcast_to(lost, (rows, LANES))
    out = jnp.concatenate([short, extra], axis=1).astype(jnp.bfloat16)
    sent[...] = jnp.broadcast_to(out[None], sent.shape)
    factor = cov_weight / feature_count / (batch_rows - 1) ** 2
    value = factor * jnp.sum(summed * summed) + jnp.sum(share[...]) + inv[0]
    scalar[...] = jnp.full(scalar.shape, value, jnp.float32)


def grad_kernel(sizes, scalar, gram, rounded, rest, sent, matrix, lost):
    batch_rows, feature_count, row_parts = sizes
    parts, rows, _ = gram.shape
    group_rows = parts * rows
    step = pl.program_id(0)
    width = rounded.shape[1]
    factor_cov = 4.0 * cov_weight * batch_rows / (batch_rows - 1) ** 2 / out_scale

    @pl.when(step == 0)
    def _():
        matrix[...] = gram[:, :, pl.ds(0, batch_rows)].reshape(group_rows, batch_rows)
        extra = gram[:, :, pl.ds(batch_rows, LANES)].reshape(group_rows, LANES)
        lost[...] = extra.astype(jnp.float32)
        value = jnp.broadcast_to(scalar[0:1], (rows, LANES))
        high = value.astype(jnp.bfloat16).astype(jnp.float32)
        middle = (value - high).astype(jnp.bfloat16).astype(jnp.float32)
        low = value - high - middle
        lane = lax.broadcasted_iota(jnp.int32, value.shape, 1)
        three = jnp.where(lane == 0, high, jnp.where(lane == 1, middle, low)).astype(jnp.bfloat16)
        whole = sent.shape[2] - LANES
        sent[:, :, pl.ds(whole, LANES)] = jnp.broadcast_to(three[None], (parts, rows, LANES))

    product = lax.dot_general(
        matrix[...], rounded[...], CONTRACT_FIRST, preferred_element_type=jnp.float32
    )
    mine = rounded[pl.ds(0, group_rows)].astype(jnp.float32)
    grad = factor_cov * (product + lost[:, 0:1] * mine) + rest[...]
    cut = pl.ds(pl.multiple_of(step * width, width), width)
    sent[:, :, cut] = grad.astype(jnp.bfloat16).reshape(parts, rows, width)


def final_kernel(core, recv, got, view_one, view_two, grad_one, grad_two, loss):
    parts, rows, width = got.shape
    width -= LANES
    push = 2.0 * inv_weight / out_scale
    sums = 0.0
    for c in range(parts):
        mine = recv[c].astype(jnp.float32)[:rows]
        other = got[c].astype(jnp.float32)
        cut = pl.ds(c * width, width)
        diff = push * (view_one[:, cut].astype(jnp.float32) - view_two[:, cut].astype(jnp.float32))
        grad_one[:, cut] = pick(core[0], mine[:, :width], other[:, :width]) + diff
        grad_two[:, cut] = pick(core[0], other[:, :width], mine[:, :width]) - diff
        sums += mine[:, width:] + other[:, width:]
    lane = lax.broadcasted_iota(jnp.int32, sums.shape, 1)
    row = lax.broadcasted_iota(jnp.int32, sums.shape, 0)
    loss[0] = jnp.sum(jnp.where((lane < 3) & (row == 0), sums, 0.0))


def body(view_one, view_two):
    shard_rows, feature_count = view_one.shape
    row_parts, feature_parts = BY_RING.shape[1:]
    batch_rows = shard_rows * 2 * row_parts * feature_parts
    group_rows = batch_rows // row_parts
    width = feature_count // feature_parts
    rows = 2 * shard_rows
    steps = 4
    chunk = width // steps
    sizes = (batch_rows, feature_count, row_parts)
    core = lax.axis_index("core")
    across = pick(core, lax.axis_index("y"), lax.axis_index("x"))
    place = (lax.axis_index("zh") * 4 + across) * 2 + lax.axis_index("zl")
    core = core.astype(jnp.int32).reshape(1)
    place = place.astype(jnp.int32).reshape(1)
    params = pltpu.CompilerParams(vmem_limit_bytes=VMEM_BYTES)
    smem = pl.BlockSpec(memory_space=pltpu.SMEM)
    vmem = pl.BlockSpec(memory_space=pltpu.VMEM)

    swapped = move(pick(core[0], view_two, view_one), SWAP)
    blocks = pl.pallas_call(
        pack_kernel,
        in_specs=[smem, vmem, vmem, vmem],
        out_specs=vmem,
        out_shape=jax.ShapeDtypeStruct((feature_parts, rows, width), jnp.bfloat16),
        compiler_params=params,
        name="pack_rows",
    )(core, view_one, view_two, swapped)
    own = exchange(blocks)
    up, down = move(own, UP), move(own, DOWN)
    half = feature_parts // 2
    far_up, far_down = move(up[:half], UP), move(down[half:], DOWN)
    view_diff = view_one.astype(jnp.float32) - view_two.astype(jnp.float32)
    inv = inv_weight / (batch_rows * feature_count) * jnp.sum(view_diff * view_diff)

    full_block = pl.BlockSpec((feature_parts, rows, chunk), lambda f: (0, 0, f))
    half_block = pl.BlockSpec((half, rows, chunk), lambda f: (0, 0, f))
    rounded, part, rest, share = pl.pallas_call(
        functools.partial(gram_kernel, sizes),
        grid=(steps,),
        in_specs=[full_block, full_block, full_block, half_block, half_block],
        out_specs=[
            pl.BlockSpec((batch_rows, chunk), lambda f: (0, f)),
            pl.BlockSpec((feature_parts, rows, batch_rows), lambda f: (0, 0, 0)),
            pl.BlockSpec((group_rows, chunk), lambda f: (0, f)),
            pl.BlockSpec((1, chunk), lambda f: (0, f)),
        ],
        scratch_shapes=[pltpu.VMEM((group_rows, batch_rows), jnp.float32)],
        out_shape=[
            jax.ShapeDtypeStruct((batch_rows, width), jnp.bfloat16),
            jax.ShapeDtypeStruct((feature_parts, rows, batch_rows), jnp.bfloat16),
            jax.ShapeDtypeStruct((group_rows, width), jnp.float32),
            jax.ShapeDtypeStruct((1, width), jnp.float32),
        ],
        compiler_params=params,
        name="gram_part",
    )(own, up, down, far_up, far_down)

    pieces = exchange(part)
    sent, scalar = pl.pallas_call(
        functools.partial(sum_kernel, sizes),
        in_specs=[smem, smem, vmem, vmem],
        out_specs=[vmem, vmem],
        out_shape=[
            jax.ShapeDtypeStruct((feature_parts, rows, batch_rows + LANES), jnp.bfloat16),
            jax.ShapeDtypeStruct((8, LANES), jnp.float32),
        ],
        compiler_params=params,
        name="gram_sum",
    )(place, inv.reshape(1), pieces, share)

    gram = exchange(sent)
    scalar = scalar + move(scalar, NEAR)
    scalar = scalar + move(scalar, FAR)

    grads = pl.pallas_call(
        functools.partial(grad_kernel, sizes),
        grid=(steps,),
        in_specs=[
            vmem,
            pl.BlockSpec(sent.shape, lambda f: (0, 0, 0)),
            pl.BlockSpec((batch_rows, chunk), lambda f: (0, f)),
            pl.BlockSpec((group_rows, chunk), lambda f: (0, f)),
        ],
        out_specs=pl.BlockSpec((feature_parts, rows, width + LANES), lambda f: (0, 0, 0)),
        out_shape=jax.ShapeDtypeStruct((feature_parts, rows, width + LANES), jnp.bfloat16),
        scratch_shapes=[
            pltpu.VMEM((group_rows, batch_rows), jnp.bfloat16),
            pltpu.VMEM((group_rows, LANES), jnp.float32),
        ],
        compiler_params=params,
        name="grad_rows",
    )(scalar, gram, rounded, rest)

    grads = exchange(grads)
    others = move(grads[:, shard_rows:], SWAP)
    grad_one, grad_two, loss = pl.pallas_call(
        final_kernel,
        in_specs=[smem, vmem, vmem, vmem, vmem],
        out_specs=[vmem, vmem, smem],
        out_shape=[
            jax.ShapeDtypeStruct(view_one.shape, jnp.float32),
            jax.ShapeDtypeStruct(view_one.shape, jnp.float32),
            jax.ShapeDtypeStruct((1,), jnp.float32),
        ],
        compiler_params=params,
        name="add_pull",
    )(core, grads, others, view_one, view_two)
    return grad_one, grad_two, loss.reshape(())


def solution(mesh):
    fine = Mesh(np.asarray(mesh.devices).reshape(SIZES), FINE)
    rows = P(FINE, None)
    return jax.shard_map(
        body, mesh=fine, in_specs=(rows, rows), out_specs=(rows, rows, P()), check_vma=False
    )
```

```python
import functools

import jax
import jax.numpy as jnp
import numpy as np
from jax import lax
from jax.experimental import pallas as pl
from jax.experimental.pallas import tpu as pltpu
from jax.sharding import Mesh
from jax.sharding import PartitionSpec as P

epsilon = 0.0001
inv_weight = 25.0
var_weight = 25.0
cov_weight = 1.0
out_scale = 25.0

FINE = ("zh", "x", "y", "zl", "core")
SIZES = (2, 4, 4, 2, 2)
LANES = 128
CONTRACT_LAST = (((1,), (1,)), ((), ()))
CONTRACT_FIRST = (((1,), (0,)), ((), ()))

IDS = np.arange(128).reshape(SIZES)
BY_RING = np.stack(
    [
        IDS[..., 0].transpose(1, 0, 2, 3).reshape(4, 16),
        IDS[..., 1].transpose(2, 0, 1, 3).reshape(4, 16),
    ]
)
GROUPS = [[int(i) for i in g] for core in BY_RING for g in core]
SWAP = [(int(i), int(i) ^ 1) for i in IDS.reshape(-1)]


def along_ring(source):
    return [
        (int(BY_RING[k, source[i], c]), int(BY_RING[k, i, c]))
        for k in range(2)
        for i in range(4)
        for c in range(16)
    ]


UP = along_ring((3, 0, 1, 2))
DOWN = along_ring((1, 2, 3, 0))
FAR = along_ring((2, 3, 0, 1))


def exchange(blocks):
    return lax.all_to_all(blocks, FINE, 0, 0, tiled=True, axis_index_groups=GROUPS)


def move(block, pairs):
    return lax.ppermute(block, FINE, pairs)


def room(mebibytes):
    return pltpu.CompilerParams(vmem_limit_bytes=mebibytes * 1024 * 1024)


def pick(core, first, second):
    return jnp.where(core == 0, first, second)


def pack_kernel(factor, keep, give, got, packed, inv):
    parts, rows, width = packed.shape
    squares = 0.0
    for c in range(parts):
        cut = pl.ds(c * width, width)
        mine, other, more = [ref[:, cut].astype(jnp.float32) for ref in (keep, give, got)]
        packed[c] = jnp.concatenate([mine, more], axis=0).astype(jnp.bfloat16)
        squares += (mine - other) ** 2
    inv[0] = factor * jnp.sum(squares)


def gram_kernel(sizes, inv, own, *refs):
    copies, (rounded, part, rest, share, total) = refs[:-5], refs[-5:]
    batch_rows, feature_count, row_parts = sizes
    group_rows = batch_rows // row_parts
    step = pl.program_id(0)
    width = own.shape[2]
    factor_cov = 4.0 * cov_weight * batch_rows / (batch_rows - 1) ** 2 / out_scale
    factor_var = var_weight * batch_rows / (batch_rows - 1) / out_scale
    values = [ref[...].reshape(-1, width).astype(jnp.float32) for ref in (own,) + copies]
    mean = sum(jnp.sum(a, axis=0, keepdims=True) for a in values) / batch_rows
    values = [a - mean for a in values]
    square = sum(jnp.sum(a * a, axis=0, keepdims=True) for a in values)
    spread = jnp.sqrt(square / (batch_rows - 1) + epsilon)
    energy = 0.0
    row = 0
    for a in values:
        a = a.astype(jnp.bfloat16)
        rounded[pl.ds(row, a.shape[0])] = a
        row += a.shape[0]
        a = a.astype(jnp.float32)
        energy += jnp.sum(a * a, axis=0, keepdims=True)
    mine = rounded[pl.ds(0, group_rows)]
    product = lax.dot_general(
        mine, rounded[...], CONTRACT_LAST, preferred_element_type=jnp.float32
    )
    hinge = values[0] * jnp.where(spread < 1.0, 1.0 / spread, 0.0)
    rest[...] = -factor_var * hinge - mine.astype(jnp.float32) * (factor_cov * energy)
    shares = var_weight / feature_count / row_parts * jnp.maximum(1.0 - spread, 0.0)
    shares += inv[0] / (width * pl.num_programs(0))
    share[...] = shares - cov_weight / feature_count / row_parts * (energy / (batch_rows - 1)) ** 2

    @pl.when(step == 0)
    def _():
        total[...] = product

    @pl.when(step > 0)
    def _():
        total[...] += product

    @pl.when(step == pl.num_programs(0) - 1)
    def _():
        part[...] = total[...].astype(jnp.bfloat16).reshape(part.shape)


def sum_kernel(sizes, place, pieces, share, sent, scalar):
    batch_rows, feature_count, row_parts = sizes
    rows = pieces.shape[1]
    summed = jnp.sum(pieces[...].astype(jnp.float32), axis=0)
    shape = summed.shape
    lane = lax.broadcasted_iota(jnp.int32, shape, 1)
    row = lax.broadcasted_iota(jnp.int32, shape, 0)
    short = summed.astype(jnp.bfloat16).astype(jnp.float32)
    on_diagonal = lane == place[0] * rows + row
    lost = jnp.sum(jnp.where(on_diagonal, summed - short, 0.0), axis=1, keepdims=True)
    extra = jnp.broadcast_to(lost, (rows, LANES))
    out = jnp.concatenate([short, extra], axis=1).astype(jnp.bfloat16)
    sent[...] = jnp.broadcast_to(out[None], sent.shape)
    factor = cov_weight / feature_count / (batch_rows - 1) ** 2
    value = factor * jnp.sum(summed * summed) + jnp.sum(share[...])
    scalar[...] = jnp.full(scalar.shape, value, jnp.float32)


def grad_kernel(sizes, here, far, before, after, gram, rounded, rest, sent, matrix, lost):
    batch_rows, feature_count, row_parts = sizes
    parts, rows, _ = gram.shape
    group_rows = parts * rows
    step = pl.program_id(0)
    width = rounded.shape[1]
    factor_cov = 4.0 * cov_weight * batch_rows / (batch_rows - 1) ** 2 / out_scale

    @pl.when(step == 0)
    def _():
        matrix[...] = gram[:, :, pl.ds(0, batch_rows)].reshape(group_rows, batch_rows)
        extra = gram[:, :, pl.ds(batch_rows, LANES)].reshape(group_rows, LANES)
        lost[...] = extra.astype(jnp.float32)
        scalar = (here[0:1] + far[0:1]) + (before[0:1] + after[0:1])
        value = jnp.broadcast_to(scalar, (rows, LANES))
        high = value.astype(jnp.bfloat16).astype(jnp.float32)
        middle = (value - high).astype(jnp.bfloat16).astype(jnp.float32)
        low = value - high - middle
        lane = lax.broadcasted_iota(jnp.int32, value.shape, 1)
        three = jnp.where(lane == 0, high, jnp.where(lane == 1, middle, low)).astype(jnp.bfloat16)
        whole = sent.shape[2] - LANES
        sent[:, :, pl.ds(whole, LANES)] = jnp.broadcast_to(three[None], (parts, rows, LANES))

    product = lax.dot_general(
        matrix[...], rounded[...], CONTRACT_FIRST, preferred_element_type=jnp.float32
    )
    mine = rounded[pl.ds(0, group_rows)].astype(jnp.float32)
    grad = factor_cov * (product + lost[:, 0:1] * mine) + rest[...]
    cut = pl.ds(pl.multiple_of(step * width, width), width)
    sent[:, :, cut] = grad.astype(jnp.bfloat16).reshape(parts, rows, width)


def final_kernel(core, recv, got, view_one, view_two, grad_one, grad_two, loss):
    parts, rows, width = got.shape
    width -= LANES
    push = 2.0 * inv_weight / out_scale
    sums = 0.0
    for c in range(parts):
        mine = recv[c].astype(jnp.float32)[:rows]
        other = got[c].astype(jnp.float32)
        cut = pl.ds(c * width, width)
        diff = push * (view_one[:, cut].astype(jnp.float32) - view_two[:, cut].astype(jnp.float32))
        grad_one[:, cut] = pick(core[0], mine[:, :width], other[:, :width]) + diff
        grad_two[:, cut] = pick(core[0], other[:, :width], mine[:, :width]) - diff
        sums += mine[:, width:] + other[:, width:]
    lane = lax.broadcasted_iota(jnp.int32, sums.shape, 1)
    row = lax.broadcasted_iota(jnp.int32, sums.shape, 0)
    loss[0] = jnp.sum(jnp.where((lane < 3) & (row == 0), sums, 0.0))


def body(view_one, view_two):
    shard_rows, feature_count = view_one.shape
    row_parts, feature_parts = BY_RING.shape[1:]
    batch_rows = shard_rows * 2 * row_parts * feature_parts
    group_rows = batch_rows // row_parts
    width = feature_count // feature_parts
    rows = 2 * shard_rows
    steps = 4
    chunk = width // steps
    sizes = (batch_rows, feature_count, row_parts)
    core = lax.axis_index("core")
    across = pick(core, lax.axis_index("y"), lax.axis_index("x"))
    place = (lax.axis_index("zh") * 4 + across) * 2 + lax.axis_index("zl")
    core = core.astype(jnp.int32).reshape(1)
    place = place.astype(jnp.int32).reshape(1)
    smem = pl.BlockSpec(memory_space=pltpu.SMEM)
    vmem = pl.BlockSpec(memory_space=pltpu.VMEM)

    keep, give = pick(core[0], view_one, view_two), pick(core[0], view_two, view_one)
    blocks, inv = pl.pallas_call(
        functools.partial(pack_kernel, inv_weight / (batch_rows * feature_count)),
        in_specs=[vmem, vmem, vmem],
        out_specs=[vmem, smem],
        out_shape=[
            jax.ShapeDtypeStruct((feature_parts, rows, width), jnp.bfloat16),
            jax.ShapeDtypeStruct((1,), jnp.float32),
        ],
        compiler_params=room(4),
        name="pack_rows",
    )(keep, give, move(give, SWAP))
    own = exchange(blocks)
    half = feature_parts // 2
    first, second = own[:half], own[half:]
    up_first, down_second = move(first, UP), move(second, DOWN)
    up_second, down_first = move(second, UP), move(first, DOWN)
    far_first, far_second = move(up_first, UP), move(down_second, DOWN)
    copies = (up_first, up_second, down_first, down_second, far_first, far_second)
    full_block = pl.BlockSpec((feature_parts, rows, chunk), lambda f: (0, 0, f))
    half_block = pl.BlockSpec((half, rows, chunk), lambda f: (0, 0, f))
    rounded, part, rest, share = pl.pallas_call(
        functools.partial(gram_kernel, sizes),
        grid=(steps,),
        in_specs=[smem, full_block] + [half_block] * len(copies),
        out_specs=[
            pl.BlockSpec((batch_rows, chunk), lambda f: (0, f)),
            pl.BlockSpec((feature_parts, rows, batch_rows), lambda f: (0, 0, 0)),
            pl.BlockSpec((group_rows, chunk), lambda f: (0, f)),
            pl.BlockSpec((1, chunk), lambda f: (0, f)),
        ],
        scratch_shapes=[pltpu.VMEM((group_rows, batch_rows), jnp.float32)],
        out_shape=[
            pltpu.HBM((batch_rows, width), jnp.bfloat16),
            pltpu.HBM((feature_parts, rows, batch_rows), jnp.bfloat16),
            jax.ShapeDtypeStruct((group_rows, width), jnp.float32),
            jax.ShapeDtypeStruct((1, width), jnp.float32),
        ],
        compiler_params=room(10),
        name="gram_part",
    )(inv, own, *copies)

    pieces = exchange(part)
    sent, scalar = pl.pallas_call(
        functools.partial(sum_kernel, sizes),
        in_specs=[smem, vmem, vmem],
        out_specs=[vmem, vmem],
        out_shape=[
            pltpu.HBM((feature_parts, rows, batch_rows + LANES), jnp.bfloat16),
            jax.ShapeDtypeStruct((8, LANES), jnp.float32),
        ],
        compiler_params=room(4),
        name="gram_sum",
    )(place, pieces, share)

    gram = exchange(sent)
    scalars = [scalar] + [move(scalar, pairs) for pairs in (FAR, UP, DOWN)]

    grads = pl.pallas_call(
        functools.partial(grad_kernel, sizes),
        grid=(steps,),
        in_specs=[vmem] * 4
        + [
            pl.BlockSpec(sent.shape, lambda f: (0, 0, 0)),
            pl.BlockSpec((batch_rows, chunk), lambda f: (0, f)),
            pl.BlockSpec((group_rows, chunk), lambda f: (0, f)),
        ],
        out_specs=pl.BlockSpec((feature_parts, rows, width + LANES), lambda f: (0, 0, 0)),
        out_shape=jax.ShapeDtypeStruct((feature_parts, rows, width + LANES), jnp.bfloat16),
        scratch_shapes=[
            pltpu.VMEM((group_rows, batch_rows), jnp.bfloat16),
            pltpu.VMEM((group_rows, LANES), jnp.float32),
        ],
        compiler_params=room(8),
        name="grad_rows",
    )(*scalars, gram, pltpu.with_memory_space_constraint(rounded, pltpu.HBM), rest)

    grads = exchange(grads)
    others = move(grads[:, shard_rows:], SWAP)
    grad_one, grad_two, loss = pl.pallas_call(
        final_kernel,
        in_specs=[smem, vmem, vmem, vmem, vmem],
        out_specs=[vmem, vmem, smem],
        out_shape=[
            jax.ShapeDtypeStruct(view_one.shape, jnp.float32),
            jax.ShapeDtypeStruct(view_one.shape, jnp.float32),
            jax.ShapeDtypeStruct((1,), jnp.float32),
        ],
        compiler_params=room(4),
        name="add_pull",
    )(core, grads, others, view_one, view_two)
    return grad_one, grad_two, loss.reshape(())


def solution(mesh):
    fine = Mesh(np.asarray(mesh.devices).reshape(SIZES), FINE)
    rows = P(FINE, None)
    return jax.shard_map(
        body, mesh=fine, in_specs=(rows, rows), out_specs=(rows, rows, P()), check_vma=False
    )
```

```python
import functools

import jax
import jax.numpy as jnp
import numpy as np
from jax import lax
from jax.experimental import pallas as pl
from jax.experimental.pallas import tpu as pltpu
from jax.sharding import Mesh
from jax.sharding import PartitionSpec as P

epsilon = 0.0001
inv_weight = 25.0
var_weight = 25.0
cov_weight = 1.0
out_scale = 25.0

FINE = ("zh", "x", "y", "zl", "core")
SIZES = (2, 4, 4, 2, 2)
LANES = 128
CHUNK = 256
CONTRACT_LAST = (((1,), (1,)), ((), ()))
CONTRACT_FIRST = (((1,), (0,)), ((), ()))

IDS = np.arange(128).reshape(SIZES)
BY_RING = np.stack(
    [
        IDS[..., 0].transpose(1, 0, 2, 3).reshape(4, 16),
        IDS[..., 1].transpose(2, 0, 1, 3).reshape(4, 16),
    ]
)
GROUPS = [[int(i) for i in g] for core in BY_RING for g in core]
SWAP = [(int(i), int(i) ^ 1) for i in IDS.reshape(-1)]


def along_ring(source):
    return [
        (int(BY_RING[k, source[i], c]), int(BY_RING[k, i, c]))
        for k in range(2)
        for i in range(4)
        for c in range(16)
    ]


UP = along_ring((3, 0, 1, 2))
DOWN = along_ring((1, 2, 3, 0))
FAR = along_ring((2, 3, 0, 1))


def exchange(blocks):
    return lax.all_to_all(blocks, FINE, 0, 0, tiled=True, axis_index_groups=GROUPS)


def move(block, pairs):
    return lax.ppermute(block, FINE, pairs)


def room(mebibytes):
    return pltpu.CompilerParams(vmem_limit_bytes=mebibytes * 1024 * 1024)


def pick(core, first, second):
    return jnp.where(core == 0, first, second)


def pack_kernel(factor, place_in, keep, give, got, packed, inv, place):
    parts, rows, width = packed.shape
    place[0] = place_in[0]
    squares = 0.0
    for c in range(parts):
        cut = pl.ds(c * width, width)
        mine, other, more = [ref[:, cut].astype(jnp.float32) for ref in (keep, give, got)]
        packed[c] = jnp.concatenate([mine, more], axis=0).astype(jnp.bfloat16)
        squares += (mine - other) ** 2
    inv[0] = factor * jnp.sum(squares)


def gram_kernel(sizes, inv, own, *refs):
    copies, (rounded, part, stats) = refs[:-3], refs[-3:]
    batch_rows, feature_count, row_parts = sizes
    group_rows = batch_rows // row_parts
    width = own.shape[2]
    for start in range(0, width, CHUNK):
        cut = pl.ds(start, CHUNK)
        values = [ref[:, :, cut].reshape(-1, CHUNK).astype(jnp.float32) for ref in (own,) + copies]
        mean = sum(jnp.sum(a, axis=0, keepdims=True) for a in values) / batch_rows
        values = [a - mean for a in values]
        square = sum(jnp.sum(a * a, axis=0, keepdims=True) for a in values)
        spread = jnp.sqrt(square / (batch_rows - 1) + epsilon)
        energy = 0.0
        row = 0
        for a in values:
            a = a.astype(jnp.bfloat16)
            rounded[pl.ds(row, a.shape[0]), cut] = a
            row += a.shape[0]
            a = a.astype(jnp.float32)
            energy += jnp.sum(a * a, axis=0, keepdims=True)
        share = var_weight / feature_count / row_parts * jnp.maximum(1.0 - spread, 0.0)
        share -= cov_weight / feature_count / row_parts * (energy / (batch_rows - 1)) ** 2
        share += inv[0] / width
        stats[0:1, cut] = mean
        stats[1:2, cut] = energy
        stats[2:3, cut] = jnp.where(spread < 1.0, 1.0 / spread, 0.0)
        stats[3:4, cut] = share
    product = lax.dot_general(
        rounded[pl.ds(0, group_rows)], rounded[...], CONTRACT_LAST, preferred_element_type=jnp.float32
    )
    part[...] = product.astype(jnp.bfloat16).reshape(part.shape)


def sum_kernel(sizes, place, pieces, stats, sent, scalar):
    batch_rows, feature_count, row_parts = sizes
    rows = pieces.shape[1]
    summed = jnp.sum(pieces[...].astype(jnp.float32), axis=0)
    shape = summed.shape
    lane = lax.broadcasted_iota(jnp.int32, shape, 1)
    row = lax.broadcasted_iota(jnp.int32, shape, 0)
    short = summed.astype(jnp.bfloat16).astype(jnp.float32)
    on_diagonal = lane == place[0] * rows + row
    lost = jnp.sum(jnp.where(on_diagonal, summed - short, 0.0), axis=1, keepdims=True)
    extra = jnp.broadcast_to(lost, (rows, LANES))
    out = jnp.concatenate([short, extra], axis=1).astype(jnp.bfloat16)
    sent[...] = jnp.broadcast_to(out[None], sent.shape)
    factor = cov_weight / feature_count / (batch_rows - 1) ** 2
    value = factor * jnp.sum(summed * summed) + jnp.sum(stats[3:4])
    scalar[...] = jnp.full(scalar.shape, value, jnp.float32)


def grad_kernel(sizes, here, far, before, after, gram, rounded, own, stats, sent):
    batch_rows, feature_count, row_parts = sizes
    parts, rows, width = own.shape
    group_rows = parts * rows
    factor_cov = 4.0 * cov_weight * batch_rows / (batch_rows - 1) ** 2 / out_scale
    factor_var = var_weight * batch_rows / (batch_rows - 1) / out_scale
    scalar = (here[0:1] + far[0:1]) + (before[0:1] + after[0:1])
    value = jnp.broadcast_to(scalar, (rows, LANES))
    high = value.astype(jnp.bfloat16).astype(jnp.float32)
    middle = (value - high).astype(jnp.bfloat16).astype(jnp.float32)
    low = value - high - middle
    lane = lax.broadcasted_iota(jnp.int32, value.shape, 1)
    three = jnp.where(lane == 0, high, jnp.where(lane == 1, middle, low)).astype(jnp.bfloat16)
    sent[:, :, pl.ds(width, LANES)] = jnp.broadcast_to(three[None], (parts, rows, LANES))

    matrix = gram[:, :, pl.ds(0, batch_rows)].reshape(group_rows, batch_rows)
    lost = gram[:, :, pl.ds(batch_rows, LANES)].reshape(group_rows, LANES).astype(jnp.float32)[:, 0:1]
    for start in range(0, width, CHUNK):
        cut = pl.ds(start, CHUNK)
        product = lax.dot_general(
            matrix, rounded[:, cut], CONTRACT_FIRST, preferred_element_type=jnp.float32
        )
        mine = rounded[pl.ds(0, group_rows), cut].astype(jnp.float32)
        centered = own[:, :, cut].reshape(group_rows, CHUNK).astype(jnp.float32) - stats[0:1, cut]
        product = product + (lost - stats[1:2, cut]) * mine
        grad = factor_cov * product - factor_var * stats[2:3, cut] * centered
        sent[:, :, cut] = grad.astype(jnp.bfloat16).reshape(parts, rows, CHUNK)


def final_kernel(core, recv, got, view_one, view_two, grad_one, grad_two, loss):
    parts, rows, width = got.shape
    width -= LANES
    push = 2.0 * inv_weight / out_scale
    sums = 0.0
    for c in range(parts):
        mine = recv[c].astype(jnp.float32)[:rows]
        other = got[c].astype(jnp.float32)
        cut = pl.ds(c * width, width)
        diff = push * (view_one[:, cut].astype(jnp.float32) - view_two[:, cut].astype(jnp.float32))
        grad_one[:, cut] = pick(core[0], mine[:, :width], other[:, :width]) + diff
        grad_two[:, cut] = pick(core[0], other[:, :width], mine[:, :width]) - diff
        sums += mine[:, width:] + other[:, width:]
    lane = lax.broadcasted_iota(jnp.int32, sums.shape, 1)
    row = lax.broadcasted_iota(jnp.int32, sums.shape, 0)
    loss[0] = jnp.sum(jnp.where((lane < 3) & (row == 0), sums, 0.0))


def body(view_one, view_two):
    shard_rows, feature_count = view_one.shape
    row_parts, feature_parts = BY_RING.shape[1:]
    batch_rows = shard_rows * 2 * row_parts * feature_parts
    group_rows = batch_rows // row_parts
    width = feature_count // feature_parts
    rows = 2 * shard_rows
    sizes = (batch_rows, feature_count, row_parts)
    core = lax.axis_index("core")
    across = pick(core, lax.axis_index("y"), lax.axis_index("x"))
    place = (lax.axis_index("zh") * 4 + across) * 2 + lax.axis_index("zl")
    core = core.astype(jnp.int32).reshape(1)
    place = place.astype(jnp.int32).reshape(1)
    smem = pl.BlockSpec(memory_space=pltpu.SMEM)
    vmem = pl.BlockSpec(memory_space=pltpu.VMEM)

    keep, give = pick(core[0], view_one, view_two), pick(core[0], view_two, view_one)
    blocks, inv, place = pl.pallas_call(
        functools.partial(pack_kernel, inv_weight / (batch_rows * feature_count)),
        in_specs=[smem, vmem, vmem, vmem],
        out_specs=[vmem, smem, smem],
        out_shape=[
            jax.ShapeDtypeStruct((feature_parts, rows, width), jnp.bfloat16),
            jax.ShapeDtypeStruct((1,), jnp.float32),
            jax.ShapeDtypeStruct((1,), jnp.int32),
        ],
        compiler_params=room(4),
        name="pack_rows",
    )(place, keep, give, move(give, SWAP))
    own = exchange(blocks)
    half = feature_parts // 2
    first, second = own[:half], own[half:]
    up_first, down_second = move(first, UP), move(second, DOWN)
    up_second, down_first = move(second, UP), move(first, DOWN)
    far_first, far_second = move(up_first, UP), move(down_second, DOWN)
    copies = (up_first, up_second, down_first, down_second, far_first, far_second)
    rounded, part, stats = pl.pallas_call(
        functools.partial(gram_kernel, sizes),
        in_specs=[smem, vmem] + [vmem] * len(copies),
        out_specs=[vmem, vmem, vmem],
        out_shape=[
            jax.ShapeDtypeStruct((batch_rows, width), jnp.bfloat16),
            jax.ShapeDtypeStruct((feature_parts, rows, batch_rows), jnp.bfloat16),
            jax.ShapeDtypeStruct((4, width), jnp.float32),
        ],
        compiler_params=room(24),
        name="gram_part",
    )(inv, own, *copies)

    pieces = exchange(part)
    sent, scalar = pl.pallas_call(
        functools.partial(sum_kernel, sizes),
        in_specs=[smem, vmem, vmem],
        out_specs=[vmem, vmem],
        out_shape=[
            pltpu.HBM((feature_parts, rows, batch_rows + LANES), jnp.bfloat16),
            jax.ShapeDtypeStruct((8, LANES), jnp.float32),
        ],
        compiler_params=room(4),
        name="gram_sum",
    )(place, pieces, stats)

    gram = exchange(sent)
    scalars = [scalar] + [move(scalar, pairs) for pairs in (FAR, UP, DOWN)]

    grads = pl.pallas_call(
        functools.partial(grad_kernel, sizes),
        in_specs=[vmem] * 8,
        out_specs=vmem,
        out_shape=jax.ShapeDtypeStruct((feature_parts, rows, width + LANES), jnp.bfloat16),
        compiler_params=room(16),
        name="grad_rows",
    )(*scalars, gram, rounded, own, stats)

    grads = exchange(grads)
    others = move(grads[:, shard_rows:], SWAP)
    grad_one, grad_two, loss = pl.pallas_call(
        final_kernel,
        in_specs=[smem, vmem, vmem, vmem, vmem],
        out_specs=[vmem, vmem, smem],
        out_shape=[
            jax.ShapeDtypeStruct(view_one.shape, jnp.float32),
            jax.ShapeDtypeStruct(view_one.shape, jnp.float32),
            jax.ShapeDtypeStruct((1,), jnp.float32),
        ],
        compiler_params=room(4),
        name="add_pull",
    )(core, grads, others, view_one, view_two)
    return grad_one, grad_two, loss.reshape(())


def solution(mesh):
    fine = Mesh(np.asarray(mesh.devices).reshape(SIZES), FINE)
    rows = P(FINE, None)
    return jax.shard_map(
        body, mesh=fine, in_specs=(rows, rows), out_specs=(rows, rows, P()), check_vma=False
    )
```

```python
import functools

import jax
import jax.numpy as jnp
import numpy as np
from jax import lax
from jax.experimental import pallas as pl
from jax.experimental.pallas import tpu as pltpu
from jax.sharding import Mesh
from jax.sharding import PartitionSpec as P

epsilon = 0.0001
inv_weight = 25.0
var_weight = 25.0
cov_weight = 1.0
out_scale = 25.0

FINE = ("zh", "x", "y", "zl", "core")
SIZES = (2, 4, 4, 2, 2)
LANES = 128
CHUNK = 256
CONTRACT_LAST = (((1,), (1,)), ((), ()))
CONTRACT_FIRST = (((1,), (0,)), ((), ()))

IDS = np.arange(128).reshape(SIZES)
BY_RING = np.stack(
    [
        IDS[..., 0].transpose(1, 0, 2, 3).reshape(4, 16),
        IDS[..., 1].transpose(2, 0, 1, 3).reshape(4, 16),
    ]
)
GROUPS = [[int(i) for i in g] for core in BY_RING for g in core]
SWAP = [(int(i), int(i) ^ 1) for i in IDS.reshape(-1)]


def along_ring(source):
    return [
        (int(BY_RING[k, source[i], c]), int(BY_RING[k, i, c]))
        for k in range(2)
        for i in range(4)
        for c in range(16)
    ]


UP = along_ring((3, 0, 1, 2))
DOWN = along_ring((1, 2, 3, 0))
FAR = along_ring((2, 3, 0, 1))


def exchange(blocks):
    return lax.all_to_all(blocks, FINE, 0, 0, tiled=True, axis_index_groups=GROUPS)


def move(block, pairs):
    return lax.ppermute(block, FINE, pairs)


def room(mebibytes):
    return pltpu.CompilerParams(vmem_limit_bytes=mebibytes * 1024 * 1024)


def pick(core, first, second):
    return jnp.where(core == 0, first, second)


def pack_kernel(factor, place_in, keep, give, got, packed, squares, place):
    parts, rows, width = packed.shape
    place[0] = place_in[0]
    total = 0.0
    for c in range(parts):
        cut = pl.ds(c * width, width)
        mine, other, more = [ref[:, cut].astype(jnp.float32) for ref in (keep, give, got)]
        packed[c] = jnp.concatenate([mine, more], axis=0).astype(jnp.bfloat16)
        total += (mine - other) ** 2
    squares[...] = factor * total


def gram_kernel(sizes, pull, own, *refs):
    copies, (rounded, part, stats) = refs[:-3], refs[-3:]
    batch_rows, feature_count, row_parts = sizes
    group_rows = batch_rows // row_parts
    width = own.shape[2]
    for start in range(0, width, CHUNK):
        cut = pl.ds(start, CHUNK)
        values = [ref[:, :, cut].reshape(-1, CHUNK).astype(jnp.float32) for ref in (own,) + copies]
        mean = sum(jnp.sum(a, axis=0, keepdims=True) for a in values) / batch_rows
        values = [a - mean for a in values]
        square = sum(jnp.sum(a * a, axis=0, keepdims=True) for a in values)
        spread = jnp.sqrt(square / (batch_rows - 1) + epsilon)
        energy = 0.0
        row = 0
        for a in values:
            a = a.astype(jnp.bfloat16)
            rounded[pl.ds(row, a.shape[0]), cut] = a
            row += a.shape[0]
            a = a.astype(jnp.float32)
            energy += jnp.sum(a * a, axis=0, keepdims=True)
        share = var_weight / feature_count / row_parts * jnp.maximum(1.0 - spread, 0.0)
        share -= cov_weight / feature_count / row_parts * (energy / (batch_rows - 1)) ** 2
        share += jnp.sum(pull[:, cut], axis=0, keepdims=True)
        stats[0:1, cut] = mean
        stats[1:2, cut] = energy
        stats[2:3, cut] = jnp.where(spread < 1.0, 1.0 / spread, 0.0)
        stats[3:4, cut] = share
    product = lax.dot_general(
        rounded[pl.ds(0, group_rows)], rounded[...], CONTRACT_LAST, preferred_element_type=jnp.float32
    )
    part[...] = product.astype(jnp.bfloat16).reshape(part.shape)


def slots(shape, rows, first, shift):
    row = lax.broadcasted_iota(jnp.int32, shape, 0)
    lane = lax.broadcasted_iota(jnp.int32, shape, 1)
    inside = row % rows
    return lane == first + row - inside + (inside + shift) % rows


def three_parts(value, shape):
    value = jnp.full(shape, value, jnp.float32)
    high = value.astype(jnp.bfloat16).astype(jnp.float32)
    middle = (value - high).astype(jnp.bfloat16).astype(jnp.float32)
    row = lax.broadcasted_iota(jnp.int32, shape, 0)
    low = jnp.where(row == 2, value - high - middle, 0.0)
    return jnp.where(row == 0, high, jnp.where(row == 1, middle, low))


def sum_kernel(sizes, place, pieces, stats, sent):
    batch_rows, feature_count, row_parts = sizes
    rows = pieces.shape[1]
    summed = jnp.sum(pieces[...].astype(jnp.float32), axis=0)
    shape = summed.shape
    first = place[0] * rows
    short = summed.astype(jnp.bfloat16).astype(jnp.float32)
    diagonal = slots(shape, rows, first, 0)
    lost = jnp.sum(jnp.where(diagonal, summed - short, 0.0), axis=1, keepdims=True)
    factor = cov_weight / feature_count / (batch_rows - 1) ** 2
    value = jnp.sum(factor * jnp.sum(summed * summed, axis=0, keepdims=True) + stats[3:4])
    out = jnp.where(slots(shape, rows, first, rows - 1), lost, short)
    out = jnp.where(slots(shape, rows, first, rows - 2), three_parts(value, (rows, 1)), out)
    sent[...] = jnp.broadcast_to(out.astype(jnp.bfloat16)[None], sent.shape)


def grad_kernel(sizes, gram, rounded, own, stats, sent, scalar):
    batch_rows, feature_count, row_parts = sizes
    parts, rows, width = own.shape
    group_rows = parts * rows
    factor_cov = 4.0 * cov_weight * batch_rows / (batch_rows - 1) ** 2 / out_scale
    factor_var = var_weight * batch_rows / (batch_rows - 1) / out_scale

    square = gram[:, :, pl.ds(0, group_rows)].reshape(group_rows, group_rows).astype(jnp.float32)
    shape = square.shape
    lane = lax.broadcasted_iota(jnp.int32, (1, group_rows), 1) % rows
    restored = square
    for shift in (1, 2):
        mirror = jnp.sum(
            jnp.where(slots(shape, rows, 0, shift), square, 0.0), axis=0, keepdims=True
        )
        ahead = pltpu.roll(mirror, group_rows - shift, 1)
        around = pltpu.roll(mirror, rows - shift, 1)
        mirror = jnp.where(lane < rows - shift, ahead, around)
        here = slots(shape, rows, 0, rows - shift)
        restored = jnp.where(here, mirror, restored)
        taken = jnp.sum(jnp.where(here, square, 0.0), axis=1, keepdims=True)
        if shift == 1:
            lost = taken
        else:
            scalar[...] = jnp.full(scalar.shape, jnp.sum(taken), jnp.float32)
    left = restored.astype(jnp.bfloat16)
    right = gram[:, :, pl.ds(group_rows, batch_rows - group_rows)]
    right = right.reshape(group_rows, batch_rows - group_rows)
    for start in range(0, width, CHUNK):
        cut = pl.ds(start, CHUNK)
        product = lax.dot_general(
            left, rounded[pl.ds(0, group_rows), cut], CONTRACT_FIRST, preferred_element_type=jnp.float32
        )
        product += lax.dot_general(
            right,
            rounded[pl.ds(group_rows, batch_rows - group_rows), cut],
            CONTRACT_FIRST,
            preferred_element_type=jnp.float32,
        )
        mine = rounded[pl.ds(0, group_rows), cut].astype(jnp.float32)
        centered = own[:, :, cut].reshape(group_rows, CHUNK).astype(jnp.float32) - stats[0:1, cut]
        product = product + (lost - stats[1:2, cut]) * mine
        grad = factor_cov * product - factor_var * stats[2:3, cut] * centered
        sent[:, :, cut] = grad.astype(jnp.bfloat16).reshape(parts, rows, CHUNK)


def final_kernel(core, recv, got, mine, other, view_one, view_two, grad_one, grad_two, loss):
    parts, rows, width = got.shape
    push = 2.0 * inv_weight / out_scale
    for c in range(parts):
        own_rows = recv[c].astype(jnp.float32)[:rows]
        more = got[c].astype(jnp.float32)
        cut = pl.ds(c * width, width)
        diff = push * (view_one[:, cut].astype(jnp.float32) - view_two[:, cut].astype(jnp.float32))
        grad_one[:, cut] = pick(core[0], own_rows, more) + diff
        grad_two[:, cut] = pick(core[0], more, own_rows) - diff
    loss[0] = jnp.max(mine[...] + other[...])


def body(view_one, view_two):
    shard_rows, feature_count = view_one.shape
    row_parts, feature_parts = BY_RING.shape[1:]
    batch_rows = shard_rows * 2 * row_parts * feature_parts
    group_rows = batch_rows // row_parts
    width = feature_count // feature_parts
    rows = 2 * shard_rows
    sizes = (batch_rows, feature_count, row_parts)
    core = lax.axis_index("core")
    across = pick(core, lax.axis_index("y"), lax.axis_index("x"))
    place = (lax.axis_index("zh") * 4 + across) * 2 + lax.axis_index("zl")
    core = core.astype(jnp.int32).reshape(1)
    place = place.astype(jnp.int32).reshape(1)
    smem = pl.BlockSpec(memory_space=pltpu.SMEM)
    vmem = pl.BlockSpec(memory_space=pltpu.VMEM)

    keep, give = pick(core[0], view_one, view_two), pick(core[0], view_two, view_one)
    blocks, pull, place = pl.pallas_call(
        functools.partial(pack_kernel, inv_weight / (batch_rows * feature_count)),
        in_specs=[smem, vmem, vmem, vmem],
        out_specs=[vmem, vmem, smem],
        out_shape=[
            jax.ShapeDtypeStruct((feature_parts, rows, width), jnp.bfloat16),
            jax.ShapeDtypeStruct((shard_rows, width), jnp.float32),
            jax.ShapeDtypeStruct((1,), jnp.int32),
        ],
        compiler_params=room(4),
        name="pack_rows",
    )(place, keep, give, move(give, SWAP))
    own = exchange(blocks)
    half = feature_parts // 2
    first, second = own[:half], own[half:]
    up_first, down_second = move(first, UP), move(second, DOWN)
    up_second, down_first = move(second, UP), move(first, DOWN)
    far_first, far_second = move(up_first, UP), move(down_second, DOWN)
    copies = (up_first, up_second, down_first, down_second, far_first, far_second)
    rounded, part, stats = pl.pallas_call(
        functools.partial(gram_kernel, sizes),
        in_specs=[vmem] * (2 + len(copies)),
        out_specs=[vmem, vmem, vmem],
        out_shape=[
            jax.ShapeDtypeStruct((batch_rows, width), jnp.bfloat16),
            jax.ShapeDtypeStruct((feature_parts, rows, batch_rows), jnp.bfloat16),
            jax.ShapeDtypeStruct((4, width), jnp.float32),
        ],
        compiler_params=room(24),
        name="gram_part",
    )(pull, own, *copies)

    pieces = exchange(part)
    sent = pl.pallas_call(
        functools.partial(sum_kernel, sizes),
        in_specs=[smem, vmem, vmem],
        out_specs=vmem,
        out_shape=jax.ShapeDtypeStruct((feature_parts, rows, batch_rows), jnp.bfloat16),
        compiler_params=room(4),
        name="gram_sum",
    )(place, pieces, stats)

    gram = exchange(sent)
    grads, scalar = pl.pallas_call(
        functools.partial(grad_kernel, sizes),
        in_specs=[vmem] * 4,
        out_specs=[vmem] * 2,
        out_shape=[
            pltpu.HBM((feature_parts, rows, width), jnp.bfloat16),
            jax.ShapeDtypeStruct((8, LANES), jnp.float32),
        ],
        compiler_params=room(16),
        name="grad_rows",
    )(gram, rounded, own, stats)

    grads = exchange(grads)
    far, before, after = [move(scalar, pairs) for pairs in (FAR, UP, DOWN)]
    scalar = (scalar + far) + (before + after)
    cut, scalar = lax.optimization_barrier((grads[:, shard_rows:], scalar))
    others, other_scalar = move(cut, SWAP), move(scalar, SWAP)
    grad_one, grad_two, loss = pl.pallas_call(
        final_kernel,
        in_specs=[smem] + [vmem] * 6,
        out_specs=[vmem, vmem, smem],
        out_shape=[
            jax.ShapeDtypeStruct(view_one.shape, jnp.float32),
            jax.ShapeDtypeStruct(view_one.shape, jnp.float32),
            jax.ShapeDtypeStruct((1,), jnp.float32),
        ],
        compiler_params=room(4),
        name="add_pull",
    )(core, grads, others, scalar, other_scalar, view_one, view_two)
    return grad_one, grad_two, loss.reshape(())


def solution(mesh):
    fine = Mesh(np.asarray(mesh.devices).reshape(SIZES), FINE)
    rows = P(FINE, None)
    return jax.shard_map(
        body, mesh=fine, in_specs=(rows, rows), out_specs=(rows, rows, P()), check_vma=False
    )
```

```python
import functools

import jax
import jax.numpy as jnp
import numpy as np
from jax import lax
from jax.experimental import pallas as pl
from jax.experimental.pallas import tpu as pltpu
from jax.sharding import Mesh
from jax.sharding import PartitionSpec as P

epsilon = 0.0001
inv_weight = 25.0
var_weight = 25.0
cov_weight = 1.0
out_scale = 25.0

FINE = ("zh", "x", "y", "zl", "core")
SIZES = (2, 4, 4, 2, 2)
LANES = 128
CHUNK = 512
CONTRACT_LAST = (((1,), (1,)), ((), ()))
CONTRACT_FIRST = (((1,), (0,)), ((), ()))

IDS = np.arange(128).reshape(SIZES)
BY_RING = np.stack(
    [
        IDS[..., 0].transpose(1, 0, 2, 3).reshape(4, 16),
        IDS[..., 1].transpose(2, 0, 1, 3).reshape(4, 16),
    ]
)
GROUPS = [[int(i) for i in g] for core in BY_RING for g in core]
SWAP = [(int(i), int(i) ^ 1) for i in IDS.reshape(-1)]


def along_ring(source):
    return [
        (int(BY_RING[k, source[i], c]), int(BY_RING[k, i, c]))
        for k in range(2)
        for i in range(4)
        for c in range(16)
    ]


UP = along_ring((3, 0, 1, 2))
DOWN = along_ring((1, 2, 3, 0))
FAR = along_ring((2, 3, 0, 1))


def exchange(blocks):
    return lax.all_to_all(blocks, FINE, 0, 0, tiled=True, axis_index_groups=GROUPS)


def move(block, pairs):
    return lax.ppermute(block, FINE, pairs)


def room(mebibytes):
    return pltpu.CompilerParams(vmem_limit_bytes=mebibytes * 1024 * 1024)


def pick(core, first, second):
    return jnp.where(core == 0, first, second)


def choose_kernel(
    factor, core, place_in, view_one, view_two, keep, squares, place, here, sems
):
    place[0] = place_in[0]
    copies = [
        pltpu.make_async_copy(view, here.at[v], sems.at[v])
        for v, view in enumerate((view_one, view_two))
    ]
    for copy in copies:
        copy.start()
    for copy in copies:
        copy.wait()
    width = squares.shape[1]
    total = 0.0
    for start in range(0, keep.shape[1], width):
        cut = pl.ds(start, width)
        first = here[0, :, cut].astype(jnp.float32)
        second = here[1, :, cut].astype(jnp.float32)
        keep[:, cut] = pick(core[0], first, second).astype(jnp.bfloat16)
        total += (first - second) ** 2
    squares[...] = factor * total


def pack_kernel(core, keep, got_one, got_two, packed):
    parts, rows, width = packed.shape
    for c in range(parts):
        cut = pl.ds(c * width, width)
        mine, first, second = [ref[:, cut].astype(jnp.float32) for ref in (keep, got_one, got_two)]
        more = pick(core[0], first, second)
        packed[c] = jnp.concatenate([mine, more], axis=0).astype(jnp.bfloat16)


def gram_kernel(sizes, pull, own, *refs):
    copies, (rounded, part, stats) = refs[:-3], refs[-3:]
    batch_rows, feature_count, row_parts = sizes
    group_rows = batch_rows // row_parts
    width = own.shape[2]
    for start in range(0, width, CHUNK):
        cut = pl.ds(start, CHUNK)
        values = [ref[:, :, cut].reshape(-1, CHUNK).astype(jnp.float32) for ref in (own,) + copies]
        mean = sum(jnp.sum(a, axis=0, keepdims=True) for a in values) / batch_rows
        values = [a - mean for a in values]
        square = sum(jnp.sum(a * a, axis=0, keepdims=True) for a in values)
        spread = jnp.sqrt(square / (batch_rows - 1) + epsilon)
        energy = 0.0
        row = 0
        for a in values:
            a = a.astype(jnp.bfloat16)
            rounded[pl.ds(row, a.shape[0]), cut] = a
            row += a.shape[0]
            a = a.astype(jnp.float32)
            energy += jnp.sum(a * a, axis=0, keepdims=True)
        share = var_weight / feature_count / row_parts * jnp.maximum(1.0 - spread, 0.0)
        share -= cov_weight / feature_count / row_parts * (energy / (batch_rows - 1)) ** 2
        share += jnp.sum(pull[:, cut], axis=0, keepdims=True)
        stats[0:1, cut] = mean
        stats[1:2, cut] = energy
        stats[2:3, cut] = jnp.where(spread < 1.0, 1.0 / spread, 0.0)
        stats[3:4, cut] = share
    product = lax.dot_general(
        rounded[pl.ds(0, group_rows)], rounded[...], CONTRACT_LAST, preferred_element_type=jnp.float32
    )
    part[...] = product.astype(jnp.bfloat16).reshape(part.shape)


def slots(shape, rows, first, shift):
    row = lax.broadcasted_iota(jnp.int32, shape, 0)
    lane = lax.broadcasted_iota(jnp.int32, shape, 1)
    inside = row % rows
    return lane == first + row - inside + (inside + shift) % rows


def three_parts(value, shape):
    value = jnp.full(shape, value, jnp.float32)
    high = value.astype(jnp.bfloat16).astype(jnp.float32)
    middle = (value - high).astype(jnp.bfloat16).astype(jnp.float32)
    row = lax.broadcasted_iota(jnp.int32, shape, 0)
    low = jnp.where(row == 2, value - high - middle, 0.0)
    return jnp.where(row == 0, high, jnp.where(row == 1, middle, low))


def sum_kernel(sizes, place, pieces, stats, sent):
    batch_rows, feature_count, row_parts = sizes
    rows = pieces.shape[1]
    summed = jnp.sum(pieces[...].astype(jnp.float32), axis=0)
    shape = summed.shape
    first = place[0] * rows
    short = summed.astype(jnp.bfloat16).astype(jnp.float32)
    diagonal = slots(shape, rows, first, 0)
    lost = jnp.sum(jnp.where(diagonal, summed - short, 0.0), axis=1, keepdims=True)
    factor = cov_weight / feature_count / (batch_rows - 1) ** 2
    value = jnp.sum(factor * jnp.sum(summed * summed, axis=0, keepdims=True) + stats[3:4])
    out = jnp.where(slots(shape, rows, first, rows - 1), lost, short)
    out = jnp.where(slots(shape, rows, first, rows - 2), three_parts(value, (rows, 1)), out)
    sent[...] = jnp.broadcast_to(out.astype(jnp.bfloat16)[None], sent.shape)


def grad_kernel(sizes, gram, rounded, own, stats, sent, scalar):
    batch_rows, feature_count, row_parts = sizes
    parts, rows, width = own.shape
    group_rows = parts * rows
    factor_cov = 4.0 * cov_weight * batch_rows / (batch_rows - 1) ** 2 / out_scale
    factor_var = var_weight * batch_rows / (batch_rows - 1) / out_scale

    square = gram[:, :, pl.ds(0, group_rows)].reshape(group_rows, group_rows).astype(jnp.float32)
    shape = square.shape
    lane = lax.broadcasted_iota(jnp.int32, (1, group_rows), 1) % rows
    restored = square
    for shift in (1, 2):
        mirror = jnp.sum(
            jnp.where(slots(shape, rows, 0, shift), square, 0.0), axis=0, keepdims=True
        )
        ahead = pltpu.roll(mirror, group_rows - shift, 1)
        around = pltpu.roll(mirror, rows - shift, 1)
        mirror = jnp.where(lane < rows - shift, ahead, around)
        here = slots(shape, rows, 0, rows - shift)
        restored = jnp.where(here, mirror, restored)
        taken = jnp.sum(jnp.where(here, square, 0.0), axis=1, keepdims=True)
        if shift == 1:
            lost = taken
        else:
            scalar[...] = jnp.full(scalar.shape, jnp.sum(taken), jnp.float32)
    left = restored.astype(jnp.bfloat16)
    right = gram[:, :, pl.ds(group_rows, batch_rows - group_rows)]
    right = right.reshape(group_rows, batch_rows - group_rows)
    for start in range(0, width, CHUNK):
        cut = pl.ds(start, CHUNK)
        product = lax.dot_general(
            left, rounded[pl.ds(0, group_rows), cut], CONTRACT_FIRST, preferred_element_type=jnp.float32
        )
        product += lax.dot_general(
            right,
            rounded[pl.ds(group_rows, batch_rows - group_rows), cut],
            CONTRACT_FIRST,
            preferred_element_type=jnp.float32,
        )
        mine = rounded[pl.ds(0, group_rows), cut].astype(jnp.float32)
        centered = own[:, :, cut].reshape(group_rows, CHUNK).astype(jnp.float32) - stats[0:1, cut]
        product = product + (lost - stats[1:2, cut]) * mine
        grad = factor_cov * product - factor_var * stats[2:3, cut] * centered
        sent[:, :, cut] = grad.astype(jnp.bfloat16).reshape(parts, rows, CHUNK)


def final_kernel(core, recv, got, mine, other, view_one, view_two, grad_one, grad_two, loss):
    parts, rows, width = got.shape
    push = 2.0 * inv_weight / out_scale
    for c in range(parts):
        own_rows = recv[c].astype(jnp.float32)[:rows]
        more = got[c].astype(jnp.float32)
        cut = pl.ds(c * width, width)
        diff = push * (view_one[:, cut].astype(jnp.float32) - view_two[:, cut].astype(jnp.float32))
        grad_one[:, cut] = pick(core[0], own_rows, more) + diff
        grad_two[:, cut] = pick(core[0], more, own_rows) - diff
    loss[0] = jnp.max(mine[...] + other[...])


def body(view_one, view_two):
    shard_rows, feature_count = view_one.shape
    row_parts, feature_parts = BY_RING.shape[1:]
    batch_rows = shard_rows * 2 * row_parts * feature_parts
    group_rows = batch_rows // row_parts
    width = feature_count // feature_parts
    rows = 2 * shard_rows
    sizes = (batch_rows, feature_count, row_parts)
    core = lax.axis_index("core")
    across = pick(core, lax.axis_index("y"), lax.axis_index("x"))
    place = (lax.axis_index("zh") * 4 + across) * 2 + lax.axis_index("zl")
    core = core.astype(jnp.int32).reshape(1)
    place = place.astype(jnp.int32).reshape(1)
    smem = pl.BlockSpec(memory_space=pltpu.SMEM)
    vmem = pl.BlockSpec(memory_space=pltpu.VMEM)
    hbm = pl.BlockSpec(memory_space=pltpu.HBM)

    got_one, got_two = move(view_one, SWAP), move(view_two, SWAP)
    keep, pull, place = pl.pallas_call(
        functools.partial(choose_kernel, inv_weight / (batch_rows * feature_count)),
        in_specs=[smem, smem, hbm, hbm],
        out_specs=[vmem, vmem, smem],
        scratch_shapes=[
            pltpu.VMEM((2,) + view_one.shape, jnp.bfloat16),
            pltpu.SemaphoreType.DMA((2,)),
        ],
        out_shape=[
            jax.ShapeDtypeStruct(view_one.shape, jnp.bfloat16),
            jax.ShapeDtypeStruct((shard_rows, width), jnp.float32),
            jax.ShapeDtypeStruct((1,), jnp.int32),
        ],
        compiler_params=room(4),
        name="choose_view",
    )(core, place, *[pltpu.with_memory_space_constraint(v, pltpu.HBM) for v in (view_one, view_two)])
    blocks = pl.pallas_call(
        pack_kernel,
        in_specs=[smem, vmem, vmem, vmem],
        out_specs=vmem,
        out_shape=jax.ShapeDtypeStruct((feature_parts, rows, width), jnp.bfloat16),
        compiler_params=room(4),
        name="pack_rows",
    )(core, keep, got_one, got_two)
    own = exchange(blocks)
    half = feature_parts // 2
    first, second = own[:half], own[half:]
    up_first, down_second = move(first, UP), move(second, DOWN)
    up_second, down_first = move(second, UP), move(first, DOWN)
    far_first, far_second = move(up_first, UP), move(down_second, DOWN)
    copies = (up_first, up_second, down_first, down_second, far_first, far_second)
    rounded, part, stats = pl.pallas_call(
        functools.partial(gram_kernel, sizes),
        in_specs=[vmem] * (2 + len(copies)),
        out_specs=[vmem, vmem, vmem],
        out_shape=[
            jax.ShapeDtypeStruct((batch_rows, width), jnp.bfloat16),
            jax.ShapeDtypeStruct((feature_parts, rows, batch_rows), jnp.bfloat16),
            jax.ShapeDtypeStruct((4, width), jnp.float32),
        ],
        compiler_params=room(24),
        name="gram_part",
    )(pull, own, *copies)

    pieces = exchange(part)
    sent = pl.pallas_call(
        functools.partial(sum_kernel, sizes),
        in_specs=[smem, vmem, vmem],
        out_specs=vmem,
        out_shape=jax.ShapeDtypeStruct((feature_parts, rows, batch_rows), jnp.bfloat16),
        compiler_params=room(4),
        name="gram_sum",
    )(place, pieces, stats)

    gram = exchange(sent)
    grads, scalar = pl.pallas_call(
        functools.partial(grad_kernel, sizes),
        in_specs=[vmem] * 4,
        out_specs=[vmem] * 2,
        out_shape=[
            pltpu.HBM((feature_parts, rows, width), jnp.bfloat16),
            jax.ShapeDtypeStruct((8, LANES), jnp.float32),
        ],
        compiler_params=room(16),
        name="grad_rows",
    )(gram, rounded, own, stats)

    grads = exchange(grads)
    far, before, after = [move(scalar, pairs) for pairs in (FAR, UP, DOWN)]
    scalar = (scalar + far) + (before + after)
    cut, scalar = lax.optimization_barrier((grads[:, shard_rows:], scalar))
    others, other_scalar = move(cut, SWAP), move(scalar, SWAP)
    grad_one, grad_two, loss = pl.pallas_call(
        final_kernel,
        in_specs=[smem] + [vmem] * 6,
        out_specs=[vmem, vmem, smem],
        out_shape=[
            jax.ShapeDtypeStruct(view_one.shape, jnp.float32),
            jax.ShapeDtypeStruct(view_one.shape, jnp.float32),
            jax.ShapeDtypeStruct((1,), jnp.float32),
        ],
        compiler_params=room(4),
        name="add_pull",
    )(core, grads, others, scalar, other_scalar, view_one, view_two)
    return grad_one, grad_two, loss.reshape(())


def solution(mesh):
    fine = Mesh(np.asarray(mesh.devices).reshape(SIZES), FINE)
    rows = P(FINE, None)
    return jax.shard_map(
        body, mesh=fine, in_specs=(rows, rows), out_specs=(rows, rows, P()), check_vma=False
    )
```

```python
import functools

import jax
import jax.numpy as jnp
import numpy as np
from jax import lax
from jax.experimental import pallas as pl
from jax.experimental.pallas import tpu as pltpu
from jax.sharding import Mesh
from jax.sharding import PartitionSpec as P

epsilon = 0.0001
inv_weight = 25.0
var_weight = 25.0
cov_weight = 1.0
out_scale = 25.0

FINE = ("zh", "x", "y", "zl", "core")
SIZES = (2, 4, 4, 2, 2)
LANES = 128
CHUNK = 512
CONTRACT_LAST = (((1,), (1,)), ((), ()))
CONTRACT_FIRST = (((1,), (0,)), ((), ()))

IDS = np.arange(128).reshape(SIZES)
BY_RING = np.stack(
    [
        IDS[..., 0].transpose(1, 0, 2, 3).reshape(4, 16),
        IDS[..., 1].transpose(2, 0, 1, 3).reshape(4, 16),
    ]
)
GROUPS = [[int(i) for i in g] for core in BY_RING for g in core]
SWAP = [(int(i), int(i) ^ 1) for i in IDS.reshape(-1)]


def along_ring(source):
    return [
        (int(BY_RING[k, source[i], c]), int(BY_RING[k, i, c]))
        for k in range(2)
        for i in range(4)
        for c in range(16)
    ]


UP = along_ring((3, 0, 1, 2))
DOWN = along_ring((1, 2, 3, 0))
FAR = along_ring((2, 3, 0, 1))


def exchange(blocks):
    return lax.all_to_all(blocks, FINE, 0, 0, tiled=True, axis_index_groups=GROUPS)


def move(block, pairs):
    return lax.ppermute(block, FINE, pairs)


def room(mebibytes):
    return pltpu.CompilerParams(vmem_limit_bytes=mebibytes * 1024 * 1024)


def pick(core, first, second):
    return jnp.where(core == 0, first, second)


def choose_kernel(
    factor, core, place_in, view_one, view_two, keep, squares, place, here, sems
):
    place[0] = place_in[0]
    copies = [
        pltpu.make_async_copy(view, here.at[v], sems.at[v])
        for v, view in enumerate((view_one, view_two))
    ]
    for copy in copies:
        copy.start()
    for copy in copies:
        copy.wait()
    width = squares.shape[1]
    total = 0.0
    for start in range(0, keep.shape[1], width):
        cut = pl.ds(start, width)
        first = here[0, :, cut].astype(jnp.float32)
        second = here[1, :, cut].astype(jnp.float32)
        keep[:, cut] = pick(core[0], first, second).astype(jnp.bfloat16)
        total += (first - second) ** 2
    squares[...] = factor * total


def pack_kernel(core, keep, got_one, got_two, packed):
    parts, rows, width = packed.shape
    for c in range(parts):
        cut = pl.ds(c * width, width)
        mine, first, second = [ref[:, cut].astype(jnp.float32) for ref in (keep, got_one, got_two)]
        more = pick(core[0], first, second)
        packed[c] = jnp.concatenate([mine, more], axis=0).astype(jnp.bfloat16)


def folded(block):
    return jnp.sum(block.reshape(-1, 8, block.shape[1]), axis=0)


def gram_kernel(sizes, pull, own, *refs):
    copies, (rounded, part, stats) = refs[:-3], refs[-3:]
    batch_rows, feature_count, row_parts = sizes
    group_rows = batch_rows // row_parts
    width = own.shape[2]
    for start in range(0, width, CHUNK):
        cut = pl.ds(start, CHUNK)
        blocks = [(ref, c) for ref in (own,) + copies for c in range(ref.shape[0])]
        total = 0.0
        for ref, c in blocks:
            total += folded(ref[c, :, cut].astype(jnp.float32))
        mean = jnp.sum(total, axis=0, keepdims=True) / batch_rows
        square, energy = 0.0, 0.0
        for i, (ref, c) in enumerate(blocks):
            a = ref[c, :, cut].astype(jnp.float32) - mean
            square += folded(a * a)
            a = a.astype(jnp.bfloat16)
            rounded[pl.ds(i * a.shape[0], a.shape[0]), cut] = a
            a = a.astype(jnp.float32)
            energy += folded(a * a)
        square = jnp.sum(square, axis=0, keepdims=True)
        energy = jnp.sum(energy, axis=0, keepdims=True)
        spread = jnp.sqrt(square / (batch_rows - 1) + epsilon)
        share = var_weight / feature_count / row_parts * jnp.maximum(1.0 - spread, 0.0)
        share -= cov_weight / feature_count / row_parts * (energy / (batch_rows - 1)) ** 2
        share += jnp.sum(pull[:, cut], axis=0, keepdims=True)
        stats[0:1, cut] = mean
        stats[1:2, cut] = energy
        stats[2:3, cut] = jnp.where(spread < 1.0, 1.0 / spread, 0.0)
        stats[3:4, cut] = share
    product = lax.dot_general(
        rounded[pl.ds(0, group_rows)], rounded[...], CONTRACT_LAST, preferred_element_type=jnp.float32
    )
    part[...] = product.astype(jnp.bfloat16).reshape(part.shape)


def slots(shape, rows, first, shift):
    row = lax.broadcasted_iota(jnp.int32, shape, 0)
    lane = lax.broadcasted_iota(jnp.int32, shape, 1)
    inside = row % rows
    return lane == first + row - inside + (inside + shift) % rows


def three_parts(value, shape):
    value = jnp.full(shape, value, jnp.float32)
    high = value.astype(jnp.bfloat16).astype(jnp.float32)
    middle = (value - high).astype(jnp.bfloat16).astype(jnp.float32)
    row = lax.broadcasted_iota(jnp.int32, shape, 0)
    low = jnp.where(row == 2, value - high - middle, 0.0)
    return jnp.where(row == 0, high, jnp.where(row == 1, middle, low))


def sum_kernel(sizes, place, pieces, stats, sent):
    batch_rows, feature_count, row_parts = sizes
    rows = pieces.shape[1]
    summed = jnp.sum(pieces[...].astype(jnp.float32), axis=0)
    shape = summed.shape
    first = place[0] * rows
    short = summed.astype(jnp.bfloat16).astype(jnp.float32)
    diagonal = slots(shape, rows, first, 0)
    lost = jnp.sum(jnp.where(diagonal, summed - short, 0.0), axis=1, keepdims=True)
    factor = cov_weight / feature_count / (batch_rows - 1) ** 2
    value = jnp.sum(factor * jnp.sum(summed * summed, axis=0, keepdims=True) + stats[3:4])
    out = jnp.where(slots(shape, rows, first, rows - 1), lost, short)
    out = jnp.where(slots(shape, rows, first, rows - 2), three_parts(value, (rows, 1)), out)
    sent[...] = jnp.broadcast_to(out.astype(jnp.bfloat16)[None], sent.shape)


def grad_kernel(sizes, gram, rounded, own, stats, sent, scalar):
    batch_rows, feature_count, row_parts = sizes
    parts, rows, width = own.shape
    group_rows = parts * rows
    factor_cov = 4.0 * cov_weight * batch_rows / (batch_rows - 1) ** 2 / out_scale
    factor_var = var_weight * batch_rows / (batch_rows - 1) / out_scale

    square = gram[:, :, pl.ds(0, group_rows)].reshape(group_rows, group_rows).astype(jnp.float32)
    shape = square.shape
    lane = lax.broadcasted_iota(jnp.int32, (1, group_rows), 1) % rows
    restored = square
    for shift in (1, 2):
        mirror = jnp.sum(
            jnp.where(slots(shape, rows, 0, shift), square, 0.0), axis=0, keepdims=True
        )
        ahead = pltpu.roll(mirror, group_rows - shift, 1)
        around = pltpu.roll(mirror, rows - shift, 1)
        mirror = jnp.where(lane < rows - shift, ahead, around)
        here = slots(shape, rows, 0, rows - shift)
        restored = jnp.where(here, mirror, restored)
        taken = jnp.sum(jnp.where(here, square, 0.0), axis=1, keepdims=True)
        if shift == 1:
            lost = taken
        else:
            scalar[...] = jnp.full(scalar.shape, jnp.sum(taken), jnp.float32)
    left = restored.astype(jnp.bfloat16)
    right = gram[:, :, pl.ds(group_rows, batch_rows - group_rows)]
    right = right.reshape(group_rows, batch_rows - group_rows)
    for start in range(0, width, CHUNK):
        cut = pl.ds(start, CHUNK)
        product = lax.dot_general(
            left, rounded[pl.ds(0, group_rows), cut], CONTRACT_FIRST, preferred_element_type=jnp.float32
        )
        product += lax.dot_general(
            right,
            rounded[pl.ds(group_rows, batch_rows - group_rows), cut],
            CONTRACT_FIRST,
            preferred_element_type=jnp.float32,
        )
        mine = rounded[pl.ds(0, group_rows), cut].astype(jnp.float32)
        centered = own[:, :, cut].reshape(group_rows, CHUNK).astype(jnp.float32) - stats[0:1, cut]
        product = product + (lost - stats[1:2, cut]) * mine
        grad = factor_cov * product - factor_var * stats[2:3, cut] * centered
        sent[:, :, cut] = grad.astype(jnp.bfloat16).reshape(parts, rows, CHUNK)


def final_kernel(core, recv, got, mine, other, view_one, view_two, grad_one, grad_two, loss):
    parts, rows, width = got.shape
    push = 2.0 * inv_weight / out_scale
    for c in range(parts):
        own_rows = recv[c].astype(jnp.float32)[:rows]
        more = got[c].astype(jnp.float32)
        cut = pl.ds(c * width, width)
        diff = push * (view_one[:, cut].astype(jnp.float32) - view_two[:, cut].astype(jnp.float32))
        grad_one[:, cut] = pick(core[0], own_rows, more) + diff
        grad_two[:, cut] = pick(core[0], more, own_rows) - diff
    loss[0] = jnp.max(mine[...] + other[...])


def body(view_one, view_two):
    shard_rows, feature_count = view_one.shape
    row_parts, feature_parts = BY_RING.shape[1:]
    batch_rows = shard_rows * 2 * row_parts * feature_parts
    group_rows = batch_rows // row_parts
    width = feature_count // feature_parts
    rows = 2 * shard_rows
    sizes = (batch_rows, feature_count, row_parts)
    core = lax.axis_index("core")
    across = pick(core, lax.axis_index("y"), lax.axis_index("x"))
    place = (lax.axis_index("zh") * 4 + across) * 2 + lax.axis_index("zl")
    core = core.astype(jnp.int32).reshape(1)
    place = place.astype(jnp.int32).reshape(1)
    smem = pl.BlockSpec(memory_space=pltpu.SMEM)
    vmem = pl.BlockSpec(memory_space=pltpu.VMEM)
    hbm = pl.BlockSpec(memory_space=pltpu.HBM)

    got_one, got_two = move(view_one, SWAP), move(view_two, SWAP)
    keep, pull, place = pl.pallas_call(
        functools.partial(choose_kernel, inv_weight / (batch_rows * feature_count)),
        in_specs=[smem, smem, hbm, hbm],
        out_specs=[vmem, vmem, smem],
        scratch_shapes=[
            pltpu.VMEM((2,) + view_one.shape, jnp.bfloat16),
            pltpu.SemaphoreType.DMA((2,)),
        ],
        out_shape=[
            jax.ShapeDtypeStruct(view_one.shape, jnp.bfloat16),
            jax.ShapeDtypeStruct((shard_rows, width), jnp.float32),
            jax.ShapeDtypeStruct((1,), jnp.int32),
        ],
        compiler_params=room(4),
        name="choose_view",
    )(core, place, *[pltpu.with_memory_space_constraint(v, pltpu.HBM) for v in (view_one, view_two)])
    blocks = pl.pallas_call(
        pack_kernel,
        in_specs=[smem, vmem, vmem, vmem],
        out_specs=vmem,
        out_shape=jax.ShapeDtypeStruct((feature_parts, rows, width), jnp.bfloat16),
        compiler_params=room(4),
        name="pack_rows",
    )(core, keep, got_one, got_two)
    own = exchange(blocks)
    copies = (move(own, UP), move(own, DOWN), move(own, FAR))

    rounded, part, stats = pl.pallas_call(
        functools.partial(gram_kernel, sizes),
        in_specs=[vmem] * (2 + len(copies)),
        out_specs=[vmem, vmem, vmem],
        out_shape=[
            jax.ShapeDtypeStruct((batch_rows, width), jnp.bfloat16),
            jax.ShapeDtypeStruct((feature_parts, rows, batch_rows), jnp.bfloat16),
            jax.ShapeDtypeStruct((4, width), jnp.float32),
        ],
        compiler_params=room(24),
        name="gram_part",
    )(pull, own, *copies)

    pieces = exchange(part)
    sent = pl.pallas_call(
        functools.partial(sum_kernel, sizes),
        in_specs=[smem, vmem, vmem],
        out_specs=vmem,
        out_shape=jax.ShapeDtypeStruct((feature_parts, rows, batch_rows), jnp.bfloat16),
        compiler_params=room(4),
        name="gram_sum",
    )(place, pieces, stats)

    gram = exchange(sent)
    grads, scalar = pl.pallas_call(
        functools.partial(grad_kernel, sizes),
        in_specs=[vmem] * 4,
        out_specs=[vmem] * 2,
        out_shape=[
            pltpu.HBM((feature_parts, rows, width), jnp.bfloat16),
            jax.ShapeDtypeStruct((8, LANES), jnp.float32),
        ],
        compiler_params=room(16),
        name="grad_rows",
    )(gram, rounded, own, stats)

    grads = exchange(grads)
    far, before, after = [move(scalar, pairs) for pairs in (FAR, UP, DOWN)]
    scalar = (scalar + far) + (before + after)
    cut, scalar = lax.optimization_barrier((grads[:, shard_rows:], scalar))
    others, other_scalar = move(cut, SWAP), move(scalar, SWAP)
    grad_one, grad_two, loss = pl.pallas_call(
        final_kernel,
        in_specs=[smem] + [vmem] * 6,
        out_specs=[vmem, vmem, smem],
        out_shape=[
            jax.ShapeDtypeStruct(view_one.shape, jnp.float32),
            jax.ShapeDtypeStruct(view_one.shape, jnp.float32),
            jax.ShapeDtypeStruct((1,), jnp.float32),
        ],
        compiler_params=room(4),
        name="add_pull",
    )(core, grads, others, scalar, other_scalar, view_one, view_two)
    return grad_one, grad_two, loss.reshape(())


def solution(mesh):
    fine = Mesh(np.asarray(mesh.devices).reshape(SIZES), FINE)
    rows = P(FINE, None)
    return jax.shard_map(
        body, mesh=fine, in_specs=(rows, rows), out_specs=(rows, rows, P()), check_vma=False
    )
```

```python
import functools

import jax
import jax.numpy as jnp
import numpy as np
from jax import lax
from jax.experimental import pallas as pl
from jax.experimental.pallas import tpu as pltpu
from jax.sharding import Mesh
from jax.sharding import PartitionSpec as P

epsilon = 0.0001
inv_weight = 25.0
var_weight = 25.0
cov_weight = 1.0
out_scale = 25.0

FINE = ("zh", "x", "y", "zl", "core")
SIZES = (2, 4, 4, 2, 2)
LANES = 128
CHUNK = 512
CONTRACT_LAST = (((1,), (1,)), ((), ()))
CONTRACT_FIRST = (((1,), (0,)), ((), ()))

IDS = np.arange(128).reshape(SIZES)
BY_RING = np.stack(
    [
        IDS[..., 0].transpose(1, 0, 2, 3).reshape(4, 16),
        IDS[..., 1].transpose(2, 0, 1, 3).reshape(4, 16),
    ]
)
GROUPS = [[int(i) for i in g] for core in BY_RING for g in core]
SWAP = [(int(i), int(i) ^ 1) for i in IDS.reshape(-1)]


def along_ring(source):
    return [
        (int(BY_RING[k, source[i], c]), int(BY_RING[k, i, c]))
        for k in range(2)
        for i in range(4)
        for c in range(16)
    ]


UP = along_ring((3, 0, 1, 2))
DOWN = along_ring((1, 2, 3, 0))
FAR = along_ring((2, 3, 0, 1))


def exchange(blocks):
    return lax.all_to_all(blocks, FINE, 0, 0, tiled=True, axis_index_groups=GROUPS)


def move(block, pairs):
    return lax.ppermute(block, FINE, pairs)


def room(mebibytes):
    return pltpu.CompilerParams(vmem_limit_bytes=mebibytes * 1024 * 1024)


def pick(core, first, second):
    return jnp.where(core == 0, first, second)


def choose_kernel(
    factor, core, place_in, view_one, view_two, keep, squares, place, here, sems
):
    place[0] = place_in[0]
    copies = [
        pltpu.make_async_copy(view, here.at[v], sems.at[v])
        for v, view in enumerate((view_one, view_two))
    ]
    for copy in copies:
        copy.start()
    for copy in copies:
        copy.wait()
    width = squares.shape[1]
    total = 0.0
    for start in range(0, keep.shape[1], width):
        cut = pl.ds(start, width)
        first = here[0, :, cut].astype(jnp.float32)
        second = here[1, :, cut].astype(jnp.float32)
        keep[:, cut] = pick(core[0], first, second).astype(jnp.bfloat16)
        total += (first - second) ** 2
    squares[...] = factor * total


def pack_kernel(core, keep, got_one, got_two, packed):
    parts, rows, width = packed.shape
    for c in range(parts):
        cut = pl.ds(c * width, width)
        mine, first, second = [ref[:, cut].astype(jnp.float32) for ref in (keep, got_one, got_two)]
        more = pick(core[0], first, second)
        packed[c] = jnp.concatenate([mine, more], axis=0).astype(jnp.bfloat16)


def folded(block):
    return jnp.sum(block.reshape(-1, 8, block.shape[1]), axis=0)


def center_kernel(sizes, pull, own, up, down, far, rounded, stats):
    copies = (up, down, far)
    batch_rows, feature_count, row_parts = sizes
    width = own.shape[2]
    for start in range(0, width, CHUNK):
        cut = pl.ds(start, CHUNK)
        blocks = [(ref, c) for ref in (own,) + copies for c in range(ref.shape[0])]
        total = 0.0
        for ref, c in blocks:
            total += folded(ref[c, :, cut].astype(jnp.float32))
        mean = jnp.sum(total, axis=0, keepdims=True) / batch_rows
        square, energy = 0.0, 0.0
        for i, (ref, c) in enumerate(blocks):
            a = ref[c, :, cut].astype(jnp.float32) - mean
            square += folded(a * a)
            a = a.astype(jnp.bfloat16)
            rounded[pl.ds(i * a.shape[0], a.shape[0]), cut] = a
            a = a.astype(jnp.float32)
            energy += folded(a * a)
        square = jnp.sum(square, axis=0, keepdims=True)
        energy = jnp.sum(energy, axis=0, keepdims=True)
        spread = jnp.sqrt(square / (batch_rows - 1) + epsilon)
        share = var_weight / feature_count / row_parts * jnp.maximum(1.0 - spread, 0.0)
        share -= cov_weight / feature_count / row_parts * (energy / (batch_rows - 1)) ** 2
        share += jnp.sum(pull[:, cut], axis=0, keepdims=True)
        stats[0:1, cut] = mean
        stats[1:2, cut] = energy
        stats[2:3, cut] = jnp.where(spread < 1.0, 1.0 / spread, 0.0)
        stats[3:4, cut] = share


def gram_kernel(sizes, pull, own, up, down, far, first, second, part, stats):
    batch_rows, feature_count, row_parts = sizes
    group_rows = batch_rows // row_parts
    center_kernel(sizes, pull, own, up, down, far, second, stats)
    product = 0.0
    for half in (first, second):
        product += lax.dot_general(
            half[pl.ds(0, group_rows)], half[...], CONTRACT_LAST, preferred_element_type=jnp.float32
        )
    part[...] = product.astype(jnp.bfloat16).reshape(part.shape)


def slots(shape, rows, first, shift):
    row = lax.broadcasted_iota(jnp.int32, shape, 0)
    lane = lax.broadcasted_iota(jnp.int32, shape, 1)
    inside = row % rows
    return lane == first + row - inside + (inside + shift) % rows


def three_parts(value, shape):
    value = jnp.full(shape, value, jnp.float32)
    high = value.astype(jnp.bfloat16).astype(jnp.float32)
    middle = (value - high).astype(jnp.bfloat16).astype(jnp.float32)
    row = lax.broadcasted_iota(jnp.int32, shape, 0)
    low = jnp.where(row == 2, value - high - middle, 0.0)
    return jnp.where(row == 0, high, jnp.where(row == 1, middle, low))


def sum_kernel(sizes, place, pieces, first_stats, second_stats, sent):
    batch_rows, feature_count, row_parts = sizes
    rows = pieces.shape[1]
    summed = jnp.sum(pieces[...].astype(jnp.float32), axis=0)
    shape = summed.shape
    first = place[0] * rows
    short = summed.astype(jnp.bfloat16).astype(jnp.float32)
    diagonal = slots(shape, rows, first, 0)
    lost = jnp.sum(jnp.where(diagonal, summed - short, 0.0), axis=1, keepdims=True)
    factor = cov_weight / feature_count / (batch_rows - 1) ** 2
    shares = jnp.concatenate([first_stats[3:4], second_stats[3:4]], axis=1)
    value = jnp.sum(factor * jnp.sum(summed * summed, axis=0, keepdims=True) + shares)
    out = jnp.where(slots(shape, rows, first, rows - 1), lost, short)
    out = jnp.where(slots(shape, rows, first, rows - 2), three_parts(value, (rows, 1)), out)
    sent[...] = jnp.broadcast_to(out.astype(jnp.bfloat16)[None], sent.shape)


def grad_kernel(
    sizes, gram, first, second, own, first_stats, second_stats, sent, scalar, left, ready, sems
):
    batch_rows, feature_count, row_parts = sizes
    parts, rows, width = own.shape
    group_rows = parts * rows
    factor_cov = 4.0 * cov_weight * batch_rows / (batch_rows - 1) ** 2 / out_scale
    factor_var = var_weight * batch_rows / (batch_rows - 1) / out_scale

    left[...] = gram[:, :, pl.ds(0, group_rows)].reshape(left.shape)
    shape = (LANES, LANES)
    lane = lax.broadcasted_iota(jnp.int32, (1, LANES), 1) % rows
    lost, shares = [], 0.0
    for start in range(0, group_rows, LANES):
        square = left[pl.ds(start, LANES), pl.ds(start, LANES)].astype(jnp.float32)
        restored = square
        for shift in (1, 2):
            mirror = jnp.where(slots(shape, rows, 0, shift), square, 0.0)
            mirror = jnp.sum(mirror, axis=0, keepdims=True)
            ahead = pltpu.roll(mirror, LANES - shift, 1)
            around = pltpu.roll(mirror, rows - shift, 1)
            mirror = jnp.where(lane < rows - shift, ahead, around)
            here = slots(shape, rows, 0, rows - shift)
            restored = jnp.where(here, mirror, restored)
            taken = jnp.where(here, square, 0.0)
            if shift == 1:
                lost.append(jnp.sum(taken, axis=1, keepdims=True))
            else:
                shares += jnp.sum(taken, axis=0, keepdims=True)
        left[pl.ds(start, LANES), pl.ds(start, LANES)] = restored.astype(jnp.bfloat16)
    lost = jnp.concatenate(lost, axis=0)
    scalar[...] = jnp.full(scalar.shape, jnp.sum(shares), jnp.float32)
    right = gram[:, :, pl.ds(group_rows, batch_rows - group_rows)]
    right = right.reshape(group_rows, batch_rows - group_rows)
    copies = []
    half = width // 2
    for i, (rounded, stats) in enumerate(((first, first_stats), (second, second_stats))):
        cut = pl.ds(i * half, half)
        product = lax.dot_general(
            left[...], rounded[pl.ds(0, group_rows)], CONTRACT_FIRST, preferred_element_type=jnp.float32
        )
        product += lax.dot_general(
            right,
            rounded[pl.ds(group_rows, batch_rows - group_rows)],
            CONTRACT_FIRST,
            preferred_element_type=jnp.float32,
        )
        mine = rounded[pl.ds(0, group_rows)].astype(jnp.float32)
        centered = own[:, :, cut].reshape(group_rows, half).astype(jnp.float32) - stats[0:1]
        product = product + (lost - stats[1:2]) * mine
        grad = factor_cov * product - factor_var * stats[2:3] * centered
        ready[i] = grad.astype(jnp.bfloat16).reshape(parts, rows, half)
        copies.append(pltpu.make_async_copy(ready.at[i], sent.at[:, :, cut], sems.at[i]))
        copies[-1].start()
    for copy in copies:
        copy.wait()


def final_kernel(core, recv, got, mine, other, view_one, view_two, grad_one, grad_two, loss):
    parts, rows, width = got.shape
    push = 2.0 * inv_weight / out_scale
    for c in range(parts):
        own_rows = recv[c].astype(jnp.float32)[:rows]
        more = got[c].astype(jnp.float32)
        cut = pl.ds(c * width, width)
        diff = push * (view_one[:, cut].astype(jnp.float32) - view_two[:, cut].astype(jnp.float32))
        grad_one[:, cut] = pick(core[0], own_rows, more) + diff
        grad_two[:, cut] = pick(core[0], more, own_rows) - diff
    loss[0] = jnp.max(mine[...] + other[...])


def body(view_one, view_two):
    shard_rows, feature_count = view_one.shape
    row_parts, feature_parts = BY_RING.shape[1:]
    batch_rows = shard_rows * 2 * row_parts * feature_parts
    group_rows = batch_rows // row_parts
    width = feature_count // feature_parts
    rows = 2 * shard_rows
    sizes = (batch_rows, feature_count, row_parts)
    core = lax.axis_index("core")
    across = pick(core, lax.axis_index("y"), lax.axis_index("x"))
    place = (lax.axis_index("zh") * 4 + across) * 2 + lax.axis_index("zl")
    core = core.astype(jnp.int32).reshape(1)
    place = place.astype(jnp.int32).reshape(1)
    smem = pl.BlockSpec(memory_space=pltpu.SMEM)
    vmem = pl.BlockSpec(memory_space=pltpu.VMEM)
    hbm = pl.BlockSpec(memory_space=pltpu.HBM)

    got_one, got_two = move(view_one, SWAP), move(view_two, SWAP)
    keep, pull, place = pl.pallas_call(
        functools.partial(choose_kernel, inv_weight / (batch_rows * feature_count)),
        in_specs=[smem, smem, hbm, hbm],
        out_specs=[vmem, vmem, smem],
        scratch_shapes=[
            pltpu.VMEM((2,) + view_one.shape, jnp.bfloat16),
            pltpu.SemaphoreType.DMA((2,)),
        ],
        out_shape=[
            jax.ShapeDtypeStruct(view_one.shape, jnp.bfloat16),
            jax.ShapeDtypeStruct((shard_rows, width), jnp.float32),
            jax.ShapeDtypeStruct((1,), jnp.int32),
        ],
        compiler_params=room(4),
        name="choose_view",
    )(core, place, *[pltpu.with_memory_space_constraint(v, pltpu.HBM) for v in (view_one, view_two)])
    blocks = pl.pallas_call(
        pack_kernel,
        in_specs=[smem, vmem, vmem, vmem],
        out_specs=vmem,
        out_shape=jax.ShapeDtypeStruct((feature_parts, rows, width), jnp.bfloat16),
        compiler_params=room(4),
        name="pack_rows",
    )(core, keep, got_one, got_two)
    own = exchange(blocks)
    half = width // 2
    halves = own[:, :, :half], own[:, :, half:]
    copies = [[move(h, pairs) for pairs in (FAR, UP, DOWN)] for h in halves]
    (far, up, down), (far_second, up_second, down_second) = copies
    rounded_shape = jax.ShapeDtypeStruct((batch_rows, half), jnp.bfloat16)
    stats_shape = jax.ShapeDtypeStruct((4, half), jnp.float32)
    first, first_stats = pl.pallas_call(
        functools.partial(center_kernel, sizes),
        in_specs=[vmem] * 5,
        out_specs=[vmem] * 2,
        out_shape=[rounded_shape, stats_shape],
        compiler_params=room(12),
        name="center_first",
    )(pull[:, :half], halves[0], up, down, far)
    second, part, second_stats = pl.pallas_call(
        functools.partial(gram_kernel, sizes),
        in_specs=[vmem] * 6,
        out_specs=[vmem] * 3,
        out_shape=[
            rounded_shape,
            jax.ShapeDtypeStruct((feature_parts, rows, batch_rows), jnp.bfloat16),
            stats_shape,
        ],
        compiler_params=room(16),
        name="gram_part",
    )(pull[:, half:], halves[1], up_second, down_second, far_second, first)

    pieces = exchange(part)
    sent = pl.pallas_call(
        functools.partial(sum_kernel, sizes),
        in_specs=[smem, vmem, vmem, vmem],
        out_specs=vmem,
        out_shape=jax.ShapeDtypeStruct((feature_parts, rows, batch_rows), jnp.bfloat16),
        compiler_params=room(4),
        name="gram_sum",
    )(place, pieces, first_stats, second_stats)

    gram = exchange(sent)
    grads, scalar = pl.pallas_call(
        functools.partial(grad_kernel, sizes),
        in_specs=[vmem] * 6,
        out_specs=[hbm, vmem],
        out_shape=[
            pltpu.HBM((feature_parts, rows, width), jnp.bfloat16),
            jax.ShapeDtypeStruct((8, LANES), jnp.float32),
        ],
        scratch_shapes=[
            pltpu.VMEM((group_rows, group_rows), jnp.bfloat16),
            pltpu.VMEM((2, feature_parts, rows, half), jnp.bfloat16),
            pltpu.SemaphoreType.DMA((2,)),
        ],
        compiler_params=room(16),
        name="grad_rows",
    )(gram, first, second, own, first_stats, second_stats)

    grads = exchange(grads)
    far, before, after = [move(scalar, pairs) for pairs in (FAR, UP, DOWN)]
    scalar = (scalar + far) + (before + after)
    cut, scalar = lax.optimization_barrier((grads[:, shard_rows:], scalar))
    others, other_scalar = move(cut, SWAP), move(scalar, SWAP)
    grad_one, grad_two, loss = pl.pallas_call(
        final_kernel,
        in_specs=[smem] + [vmem] * 6,
        out_specs=[vmem, vmem, smem],
        out_shape=[
            jax.ShapeDtypeStruct(view_one.shape, jnp.float32),
            jax.ShapeDtypeStruct(view_one.shape, jnp.float32),
            jax.ShapeDtypeStruct((1,), jnp.float32),
        ],
        compiler_params=room(4),
        name="add_pull",
    )(core, grads, others, scalar, other_scalar, view_one, view_two)
    return grad_one, grad_two, loss.reshape(())


def solution(mesh):
    fine = Mesh(np.asarray(mesh.devices).reshape(SIZES), FINE)
    rows = P(FINE, None)
    return jax.shard_map(
        body, mesh=fine, in_specs=(rows, rows), out_specs=(rows, rows, P()), check_vma=False
    )
```

```python
import functools

import jax
import jax.numpy as jnp
import numpy as np
from jax import lax
from jax.experimental import pallas as pl
from jax.experimental.pallas import tpu as pltpu
from jax.sharding import Mesh
from jax.sharding import PartitionSpec as P

epsilon = 0.0001
inv_weight = 25.0
var_weight = 25.0
cov_weight = 1.0
out_scale = 25.0

FINE = ("zh", "x", "y", "zl", "core")
SIZES = (2, 4, 4, 2, 2)
LANES = 128
CHUNK = 512
CONTRACT_LAST = (((1,), (1,)), ((), ()))
CONTRACT_FIRST = (((1,), (0,)), ((), ()))

IDS = np.arange(128).reshape(SIZES)
BY_RING = np.stack(
    [
        IDS[..., 0].transpose(1, 0, 2, 3).reshape(4, 16),
        IDS[..., 1].transpose(2, 0, 1, 3).reshape(4, 16),
    ]
)
GROUPS = [[int(i) for i in g] for core in BY_RING for g in core]
SWAP = [(int(i), int(i) ^ 1) for i in IDS.reshape(-1)]


def along_ring(source):
    return [
        (int(BY_RING[k, source[i], c]), int(BY_RING[k, i, c]))
        for k in range(2)
        for i in range(4)
        for c in range(16)
    ]


UP = along_ring((3, 0, 1, 2))
DOWN = along_ring((1, 2, 3, 0))
FAR = along_ring((2, 3, 0, 1))


def exchange(blocks):
    return lax.all_to_all(blocks, FINE, 0, 0, tiled=True, axis_index_groups=GROUPS)


def move(block, pairs):
    return lax.ppermute(block, FINE, pairs)


def room(mebibytes):
    return pltpu.CompilerParams(vmem_limit_bytes=mebibytes * 1024 * 1024)


def pick(core, first, second):
    return jnp.where(core == 0, first, second)


def choose_kernel(factor, core, place_in, view_one, view_two, keep, squares, place):
    place[0] = place_in[0]
    width = squares.shape[1]
    total = 0.0
    for start in range(0, keep.shape[1], width):
        cut = pl.ds(start, width)
        first = view_one[:, cut].astype(jnp.float32)
        second = view_two[:, cut].astype(jnp.float32)
        keep[:, cut] = pick(core[0], first, second).astype(jnp.bfloat16)
        total += (first - second) ** 2
    squares[...] = factor * total


def pack_kernel(core, keep, got_one, got_two, packed):
    parts, rows, width = packed.shape
    for c in range(parts):
        cut = pl.ds(c * width, width)
        mine, first, second = [ref[:, cut].astype(jnp.float32) for ref in (keep, got_one, got_two)]
        more = pick(core[0], first, second)
        packed[c] = jnp.concatenate([mine, more], axis=0).astype(jnp.bfloat16)


def folded(block):
    return jnp.sum(block.reshape(-1, 8, block.shape[1]), axis=0)


def center_kernel(sizes, pull, own, up, down, far, rounded, stats):
    copies = (up, down, far)
    batch_rows, feature_count, row_parts = sizes
    width = own.shape[2]
    for start in range(0, width, CHUNK):
        cut = pl.ds(start, CHUNK)
        blocks = [(ref, c) for ref in (own,) + copies for c in range(ref.shape[0])]
        total = 0.0
        for ref, c in blocks:
            total += folded(ref[c, :, cut].astype(jnp.float32))
        mean = jnp.sum(total, axis=0, keepdims=True) / batch_rows
        square, energy = 0.0, 0.0
        for i, (ref, c) in enumerate(blocks):
            a = ref[c, :, cut].astype(jnp.float32) - mean
            square += folded(a * a)
            a = a.astype(jnp.bfloat16)
            rounded[pl.ds(i * a.shape[0], a.shape[0]), cut] = a
            a = a.astype(jnp.float32)
            energy += folded(a * a)
        square = jnp.sum(square, axis=0, keepdims=True)
        energy = jnp.sum(energy, axis=0, keepdims=True)
        spread = jnp.sqrt(square / (batch_rows - 1) + epsilon)
        share = var_weight / feature_count / row_parts * jnp.maximum(1.0 - spread, 0.0)
        share -= cov_weight / feature_count / row_parts * (energy / (batch_rows - 1)) ** 2
        share += jnp.sum(pull[:, cut], axis=0, keepdims=True)
        stats[0:1, cut] = mean
        stats[1:2, cut] = energy
        stats[2:3, cut] = jnp.where(spread < 1.0, 1.0 / spread, 0.0)
        stats[3:4, cut] = share


def gram_kernel(sizes, pull, own, up, down, far, first, second, part, stats):
    batch_rows, feature_count, row_parts = sizes
    group_rows = batch_rows // row_parts
    center_kernel(sizes, pull, own, up, down, far, second, stats)
    product = 0.0
    for half in (first, second):
        product += lax.dot_general(
            half[pl.ds(0, group_rows)], half[...], CONTRACT_LAST, preferred_element_type=jnp.float32
        )
    part[...] = product.astype(jnp.bfloat16).reshape(part.shape)


def slots(shape, rows, first, shift):
    row = lax.broadcasted_iota(jnp.int32, shape, 0)
    lane = lax.broadcasted_iota(jnp.int32, shape, 1)
    inside = row % rows
    return lane == first + row - inside + (inside + shift) % rows


def three_parts(value, shape):
    value = jnp.full(shape, value, jnp.float32)
    high = value.astype(jnp.bfloat16).astype(jnp.float32)
    middle = (value - high).astype(jnp.bfloat16).astype(jnp.float32)
    row = lax.broadcasted_iota(jnp.int32, shape, 0)
    low = jnp.where(row == 2, value - high - middle, 0.0)
    return jnp.where(row == 0, high, jnp.where(row == 1, middle, low))


def sum_kernel(sizes, place, pieces, first_stats, second_stats, sent):
    batch_rows, feature_count, row_parts = sizes
    rows = pieces.shape[1]
    summed = jnp.sum(pieces[...].astype(jnp.float32), axis=0)
    shape = summed.shape
    first = place[0] * rows
    short = summed.astype(jnp.bfloat16).astype(jnp.float32)
    diagonal = slots(shape, rows, first, 0)
    lost = jnp.sum(jnp.where(diagonal, summed - short, 0.0), axis=1, keepdims=True)
    factor = cov_weight / feature_count / (batch_rows - 1) ** 2
    shares = jnp.concatenate([first_stats[3:4], second_stats[3:4]], axis=1)
    value = jnp.sum(factor * jnp.sum(summed * summed, axis=0, keepdims=True) + shares)
    out = jnp.where(slots(shape, rows, first, rows - 1), lost, short)
    out = jnp.where(slots(shape, rows, first, rows - 2), three_parts(value, (rows, 1)), out)
    sent[...] = jnp.broadcast_to(out.astype(jnp.bfloat16)[None], sent.shape)


def grad_kernel(
    sizes, gram, first, second, own, first_stats, second_stats, sent, scalar, left, ready, sems
):
    batch_rows, feature_count, row_parts = sizes
    parts, rows, width = own.shape
    group_rows = parts * rows
    factor_cov = 4.0 * cov_weight * batch_rows / (batch_rows - 1) ** 2 / out_scale
    factor_var = var_weight * batch_rows / (batch_rows - 1) / out_scale

    left[...] = gram[:, :, pl.ds(0, group_rows)].reshape(left.shape)
    shape = (LANES, LANES)
    lane = lax.broadcasted_iota(jnp.int32, (1, LANES), 1) % rows
    lost, shares = [], 0.0
    for start in range(0, group_rows, LANES):
        square = left[pl.ds(start, LANES), pl.ds(start, LANES)].astype(jnp.float32)
        restored = square
        for shift in (1, 2):
            mirror = jnp.where(slots(shape, rows, 0, shift), square, 0.0)
            mirror = jnp.sum(mirror, axis=0, keepdims=True)
            ahead = pltpu.roll(mirror, LANES - shift, 1)
            around = pltpu.roll(mirror, rows - shift, 1)
            mirror = jnp.where(lane < rows - shift, ahead, around)
            here = slots(shape, rows, 0, rows - shift)
            restored = jnp.where(here, mirror, restored)
            taken = jnp.where(here, square, 0.0)
            if shift == 1:
                lost.append(jnp.sum(taken, axis=1, keepdims=True))
            else:
                shares += jnp.sum(taken, axis=0, keepdims=True)
        left[pl.ds(start, LANES), pl.ds(start, LANES)] = restored.astype(jnp.bfloat16)
    lost = jnp.concatenate(lost, axis=0)
    scalar[...] = jnp.full(scalar.shape, jnp.sum(shares), jnp.float32)
    right = gram[:, :, pl.ds(group_rows, batch_rows - group_rows)]
    right = right.reshape(group_rows, batch_rows - group_rows)
    copies = []
    half = width // 2
    for i, (rounded, stats) in enumerate(((first, first_stats), (second, second_stats))):
        cut = pl.ds(i * half, half)
        product = lax.dot_general(
            left[...], rounded[pl.ds(0, group_rows)], CONTRACT_FIRST, preferred_element_type=jnp.float32
        )
        product += lax.dot_general(
            right,
            rounded[pl.ds(group_rows, batch_rows - group_rows)],
            CONTRACT_FIRST,
            preferred_element_type=jnp.float32,
        )
        mine = rounded[pl.ds(0, group_rows)].astype(jnp.float32)
        centered = own[:, :, cut].reshape(group_rows, half).astype(jnp.float32) - stats[0:1]
        product = product + (lost - stats[1:2]) * mine
        grad = factor_cov * product - factor_var * stats[2:3] * centered
        ready[i] = grad.astype(jnp.bfloat16).reshape(parts, rows, half)
        copies.append(pltpu.make_async_copy(ready.at[i], sent.at[:, :, cut], sems.at[i]))
        copies[-1].start()
    for copy in copies:
        copy.wait()


def final_kernel(core, recv, got, mine, other, view_one, view_two, grad_one, grad_two, loss):
    parts, rows, width = got.shape
    push = 2.0 * inv_weight / out_scale
    for c in range(parts):
        own_rows = recv[c].astype(jnp.float32)[:rows]
        more = got[c].astype(jnp.float32)
        cut = pl.ds(c * width, width)
        diff = push * (view_one[:, cut].astype(jnp.float32) - view_two[:, cut].astype(jnp.float32))
        grad_one[:, cut] = pick(core[0], own_rows, more) + diff
        grad_two[:, cut] = pick(core[0], more, own_rows) - diff
    loss[0] = jnp.max(mine[...] + other[...])


def body(view_one, view_two):
    shard_rows, feature_count = view_one.shape
    row_parts, feature_parts = BY_RING.shape[1:]
    batch_rows = shard_rows * 2 * row_parts * feature_parts
    group_rows = batch_rows // row_parts
    width = feature_count // feature_parts
    rows = 2 * shard_rows
    sizes = (batch_rows, feature_count, row_parts)
    core = lax.axis_index("core")
    across = pick(core, lax.axis_index("y"), lax.axis_index("x"))
    place = (lax.axis_index("zh") * 4 + across) * 2 + lax.axis_index("zl")
    core = core.astype(jnp.int32).reshape(1)
    place = place.astype(jnp.int32).reshape(1)
    smem = pl.BlockSpec(memory_space=pltpu.SMEM)
    vmem = pl.BlockSpec(memory_space=pltpu.VMEM)
    hbm = pl.BlockSpec(memory_space=pltpu.HBM)

    got_one, got_two = move(view_one, SWAP), move(view_two, SWAP)
    keep, pull, place = pl.pallas_call(
        functools.partial(choose_kernel, inv_weight / (batch_rows * feature_count)),
        in_specs=[smem, smem, vmem, vmem],
        out_specs=[vmem, vmem, smem],
        out_shape=[
            jax.ShapeDtypeStruct(view_one.shape, jnp.bfloat16),
            jax.ShapeDtypeStruct((shard_rows, width), jnp.float32),
            jax.ShapeDtypeStruct((1,), jnp.int32),
        ],
        compiler_params=room(4),
        name="choose_view",
    )(core, place, *[pltpu.with_memory_space_constraint(v, pltpu.HBM) for v in (view_one, view_two)])
    blocks = pl.pallas_call(
        pack_kernel,
        in_specs=[smem, vmem, vmem, vmem],
        out_specs=vmem,
        out_shape=jax.ShapeDtypeStruct((feature_parts, rows, width), jnp.bfloat16),
        compiler_params=room(4),
        name="pack_rows",
    )(core, keep, got_one, got_two)
    own = exchange(blocks)
    half = width // 2
    halves = own[:, :, :half], own[:, :, half:]
    copies = [[move(h, pairs) for pairs in (FAR, UP, DOWN)] for h in halves]
    (far, up, down), (far_second, up_second, down_second) = copies
    rounded_shape = jax.ShapeDtypeStruct((batch_rows, half), jnp.bfloat16)
    stats_shape = jax.ShapeDtypeStruct((4, half), jnp.float32)
    first, first_stats = pl.pallas_call(
        functools.partial(center_kernel, sizes),
        in_specs=[vmem] * 5,
        out_specs=[vmem] * 2,
        out_shape=[rounded_shape, stats_shape],
        compiler_params=room(12),
        name="center_first",
    )(pull[:, :half], halves[0], up, down, far)
    second, part, second_stats = pl.pallas_call(
        functools.partial(gram_kernel, sizes),
        in_specs=[vmem] * 6,
        out_specs=[vmem] * 3,
        out_shape=[
            rounded_shape,
            jax.ShapeDtypeStruct((feature_parts, rows, batch_rows), jnp.bfloat16),
            stats_shape,
        ],
        compiler_params=room(16),
        name="gram_part",
    )(pull[:, half:], halves[1], up_second, down_second, far_second, first)

    pieces = exchange(part)
    sent = pl.pallas_call(
        functools.partial(sum_kernel, sizes),
        in_specs=[smem, vmem, vmem, vmem],
        out_specs=vmem,
        out_shape=jax.ShapeDtypeStruct((feature_parts, rows, batch_rows), jnp.bfloat16),
        compiler_params=room(4),
        name="gram_sum",
    )(place, pieces, first_stats, second_stats)

    gram = exchange(sent)
    grads, scalar = pl.pallas_call(
        functools.partial(grad_kernel, sizes),
        in_specs=[vmem] * 6,
        out_specs=[hbm, vmem],
        out_shape=[
            pltpu.HBM((feature_parts, rows, width), jnp.bfloat16),
            jax.ShapeDtypeStruct((8, LANES), jnp.float32),
        ],
        scratch_shapes=[
            pltpu.VMEM((group_rows, group_rows), jnp.bfloat16),
            pltpu.VMEM((2, feature_parts, rows, half), jnp.bfloat16),
            pltpu.SemaphoreType.DMA((2,)),
        ],
        compiler_params=room(16),
        name="grad_rows",
    )(gram, first, second, own, first_stats, second_stats)

    grads = exchange(grads)
    far, before, after = [move(scalar, pairs) for pairs in (FAR, UP, DOWN)]
    scalar = (scalar + far) + (before + after)
    cut, scalar = lax.optimization_barrier((grads[:, shard_rows:], scalar))
    others, other_scalar = move(cut, SWAP), move(scalar, SWAP)
    grad_one, grad_two, loss = pl.pallas_call(
        final_kernel,
        in_specs=[smem] + [vmem] * 6,
        out_specs=[vmem, vmem, smem],
        out_shape=[
            jax.ShapeDtypeStruct(view_one.shape, jnp.float32),
            jax.ShapeDtypeStruct(view_one.shape, jnp.float32),
            jax.ShapeDtypeStruct((1,), jnp.float32),
        ],
        compiler_params=room(4),
        name="add_pull",
    )(core, grads, others, scalar, other_scalar, view_one, view_two)
    return grad_one, grad_two, loss.reshape(())


def solution(mesh):
    fine = Mesh(np.asarray(mesh.devices).reshape(SIZES), FINE)
    rows = P(FINE, None)
    return jax.shard_map(
        body, mesh=fine, in_specs=(rows, rows), out_specs=(rows, rows, P()), check_vma=False
    )
```

```python
import functools

import jax
import jax.numpy as jnp
import numpy as np
from jax import lax
from jax.experimental import pallas as pl
from jax.experimental.pallas import tpu as pltpu
from jax.sharding import Mesh
from jax.sharding import PartitionSpec as P

epsilon = 0.0001
inv_weight = 25.0
var_weight = 25.0
cov_weight = 1.0
out_scale = 25.0

FINE = ("zh", "x", "y", "zl", "core")
SIZES = (2, 4, 4, 2, 2)
LANES = 128
CHUNK = 512
CONTRACT_LAST = (((1,), (1,)), ((), ()))
CONTRACT_FIRST = (((1,), (0,)), ((), ()))

IDS = np.arange(128).reshape(SIZES)
BY_RING = np.stack(
    [
        IDS[..., 0].transpose(1, 0, 2, 3).reshape(4, 16),
        IDS[..., 1].transpose(2, 0, 1, 3).reshape(4, 16),
    ]
)
GROUPS = [[int(i) for i in g] for core in BY_RING for g in core]
SWAP = [(int(i), int(i) ^ 1) for i in IDS.reshape(-1)]


def along_ring(source):
    return [
        (int(BY_RING[k, source[i], c]), int(BY_RING[k, i, c]))
        for k in range(2)
        for i in range(4)
        for c in range(16)
    ]


UP = along_ring((3, 0, 1, 2))
DOWN = along_ring((1, 2, 3, 0))
FAR = along_ring((2, 3, 0, 1))


def exchange(blocks):
    return lax.all_to_all(blocks, FINE, 0, 0, tiled=True, axis_index_groups=GROUPS)


def move(block, pairs):
    return lax.ppermute(block, FINE, pairs)


def room(mebibytes):
    return pltpu.CompilerParams(vmem_limit_bytes=mebibytes * 1024 * 1024)


def pick(core, first, second):
    return jnp.where(core == 0, first, second)


def choose_kernel(factor, core, place_in, view_one, view_two, keep, squares, place):
    place[0] = place_in[0]
    width = squares.shape[1]
    total = 0.0
    for start in range(0, keep.shape[1], width):
        cut = pl.ds(start, width)
        first = view_one[:, cut].astype(jnp.float32)
        second = view_two[:, cut].astype(jnp.float32)
        keep[:, cut] = pick(core[0], first, second).astype(jnp.bfloat16)
        total += (first - second) ** 2
    squares[...] = factor * total


def pack_kernel(core, keep, got_one, got_two, packed):
    parts, rows, width = packed.shape
    for c in range(parts):
        cut = pl.ds(c * width, width)
        mine, first, second = [ref[:, cut].astype(jnp.float32) for ref in (keep, got_one, got_two)]
        more = pick(core[0], first, second)
        packed[c] = jnp.concatenate([mine, more], axis=0).astype(jnp.bfloat16)


def folded(block):
    return jnp.sum(block.reshape(-1, 8, block.shape[1]), axis=0)


def center_kernel(sizes, pull, own, up, down, far, rounded, stats):
    copies = (up, down, far)
    batch_rows, feature_count, row_parts = sizes
    width = own.shape[2]
    for start in range(0, width, CHUNK):
        cut = pl.ds(start, CHUNK)
        blocks = [(ref, c) for ref in (own,) + copies for c in range(ref.shape[0])]
        total = 0.0
        for ref, c in blocks:
            total += folded(ref[c, :, cut].astype(jnp.float32))
        mean = jnp.sum(total, axis=0, keepdims=True) / batch_rows
        square, energy = 0.0, 0.0
        for i, (ref, c) in enumerate(blocks):
            a = ref[c, :, cut].astype(jnp.float32) - mean
            square += folded(a * a)
            a = a.astype(jnp.bfloat16)
            rounded[pl.ds(i * a.shape[0], a.shape[0]), cut] = a
            a = a.astype(jnp.float32)
            energy += folded(a * a)
        square = jnp.sum(square, axis=0, keepdims=True)
        energy = jnp.sum(energy, axis=0, keepdims=True)
        spread = jnp.sqrt(square / (batch_rows - 1) + epsilon)
        share = var_weight / feature_count / row_parts * jnp.maximum(1.0 - spread, 0.0)
        share -= cov_weight / feature_count / row_parts * (energy / (batch_rows - 1)) ** 2
        share += jnp.sum(pull[:, cut], axis=0, keepdims=True)
        stats[0:1, cut] = mean
        stats[1:2, cut] = energy
        stats[2:3, cut] = jnp.where(spread < 1.0, 1.0 / spread, 0.0)
        stats[3:4, cut] = share


def gram_kernel(sizes, pull, own, up, down, far, first, second, part, stats):
    batch_rows, feature_count, row_parts = sizes
    group_rows = batch_rows // row_parts
    center_kernel(sizes, pull, own, up, down, far, second, stats)
    product = 0.0
    for half in (first, second):
        product += lax.dot_general(
            half[pl.ds(0, group_rows)], half[...], CONTRACT_LAST, preferred_element_type=jnp.float32
        )
    part[...] = product.astype(jnp.bfloat16).reshape(part.shape)


def slots(shape, rows, first, shift):
    row = lax.broadcasted_iota(jnp.int32, shape, 0)
    lane = lax.broadcasted_iota(jnp.int32, shape, 1)
    inside = row % rows
    return lane == first + row - inside + (inside + shift) % rows


def three_parts(value, shape):
    value = jnp.full(shape, value, jnp.float32)
    high = value.astype(jnp.bfloat16).astype(jnp.float32)
    middle = (value - high).astype(jnp.bfloat16).astype(jnp.float32)
    row = lax.broadcasted_iota(jnp.int32, shape, 0)
    low = jnp.where(row == 2, value - high - middle, 0.0)
    return jnp.where(row == 0, high, jnp.where(row == 1, middle, low))


def sum_kernel(sizes, place, pieces, first_stats, second_stats, sent):
    batch_rows, feature_count, row_parts = sizes
    rows = pieces.shape[1]
    summed = jnp.sum(pieces[...].astype(jnp.float32), axis=0)
    shape = summed.shape
    first = place[0] * rows
    short = summed.astype(jnp.bfloat16).astype(jnp.float32)
    diagonal = slots(shape, rows, first, 0)
    lost = jnp.sum(jnp.where(diagonal, summed - short, 0.0), axis=1, keepdims=True)
    factor = cov_weight / feature_count / (batch_rows - 1) ** 2
    shares = jnp.concatenate([first_stats[3:4], second_stats[3:4]], axis=1)
    value = jnp.sum(factor * jnp.sum(summed * summed, axis=0, keepdims=True) + shares)
    out = jnp.where(slots(shape, rows, first, rows - 1), lost, short)
    out = jnp.where(slots(shape, rows, first, rows - 2), three_parts(value, (rows, 1)), out)
    sent[...] = jnp.broadcast_to(out.astype(jnp.bfloat16)[None], sent.shape)


def grad_kernel(
    sizes, gram, first, second, own, first_stats, second_stats, sent, scalar, left, ready, sems
):
    batch_rows, feature_count, row_parts = sizes
    parts, rows, width = own.shape
    group_rows = parts * rows
    factor_cov = 4.0 * cov_weight * batch_rows / (batch_rows - 1) ** 2 / out_scale
    factor_var = var_weight * batch_rows / (batch_rows - 1) / out_scale

    left[...] = gram[:, :, pl.ds(0, group_rows)].reshape(left.shape)
    shape = (LANES, LANES)
    lane = lax.broadcasted_iota(jnp.int32, (1, LANES), 1) % rows
    lost, shares = [], 0.0
    for start in range(0, group_rows, LANES):
        square = left[pl.ds(start, LANES), pl.ds(start, LANES)].astype(jnp.float32)
        restored = square
        for shift in (1, 2):
            mirror = jnp.where(slots(shape, rows, 0, shift), square, 0.0)
            mirror = jnp.sum(mirror, axis=0, keepdims=True)
            ahead = pltpu.roll(mirror, LANES - shift, 1)
            around = pltpu.roll(mirror, rows - shift, 1)
            mirror = jnp.where(lane < rows - shift, ahead, around)
            here = slots(shape, rows, 0, rows - shift)
            restored = jnp.where(here, mirror, restored)
            taken = jnp.where(here, square, 0.0)
            if shift == 1:
                lost.append(jnp.sum(taken, axis=1, keepdims=True))
            else:
                shares += jnp.sum(taken, axis=0, keepdims=True)
        left[pl.ds(start, LANES), pl.ds(start, LANES)] = restored.astype(jnp.bfloat16)
    lost = jnp.concatenate(lost, axis=0)
    scalar[...] = jnp.full(scalar.shape, jnp.sum(shares), jnp.float32)
    right = gram[:, :, pl.ds(group_rows, batch_rows - group_rows)]
    right = right.reshape(group_rows, batch_rows - group_rows)
    copies = []
    half = width // 2
    for i, (rounded, stats) in enumerate(((first, first_stats), (second, second_stats))):
        cut = pl.ds(i * half, half)
        product = lax.dot_general(
            left[...], rounded[pl.ds(0, group_rows)], CONTRACT_FIRST, preferred_element_type=jnp.float32
        )
        product += lax.dot_general(
            right,
            rounded[pl.ds(group_rows, batch_rows - group_rows)],
            CONTRACT_FIRST,
            preferred_element_type=jnp.float32,
        )
        mine = rounded[pl.ds(0, group_rows)].astype(jnp.float32)
        centered = own[:, :, cut].reshape(group_rows, half).astype(jnp.float32) - stats[0:1]
        product = product + (lost - stats[1:2]) * mine
        grad = factor_cov * product - factor_var * stats[2:3] * centered
        ready[i] = grad.astype(jnp.bfloat16).reshape(parts, rows, half)
        copies.append(pltpu.make_async_copy(ready.at[i], sent.at[:, :, cut], sems.at[i]))
        copies[-1].start()
    for copy in copies:
        copy.wait()


def final_kernel(core, recv, got, mine, other, view_one, view_two, grad_one, grad_two, loss):
    parts, rows, width = got.shape
    push = 2.0 * inv_weight / out_scale
    for c in range(parts):
        own_rows = recv[c].astype(jnp.float32)[:rows]
        more = got[c].astype(jnp.float32)
        cut = pl.ds(c * width, width)
        diff = push * (view_one[:, cut].astype(jnp.float32) - view_two[:, cut].astype(jnp.float32))
        grad_one[:, cut] = pick(core[0], own_rows, more) + diff
        grad_two[:, cut] = pick(core[0], more, own_rows) - diff
    loss[0] = jnp.max(mine[...] + other[...])


def body(view_one, view_two):
    shard_rows, feature_count = view_one.shape
    row_parts, feature_parts = BY_RING.shape[1:]
    batch_rows = shard_rows * 2 * row_parts * feature_parts
    group_rows = batch_rows // row_parts
    width = feature_count // feature_parts
    rows = 2 * shard_rows
    sizes = (batch_rows, feature_count, row_parts)
    core = lax.axis_index("core")
    across = pick(core, lax.axis_index("y"), lax.axis_index("x"))
    place = (lax.axis_index("zh") * 4 + across) * 2 + lax.axis_index("zl")
    core = core.astype(jnp.int32).reshape(1)
    place = place.astype(jnp.int32).reshape(1)
    smem = pl.BlockSpec(memory_space=pltpu.SMEM)
    vmem = pl.BlockSpec(memory_space=pltpu.VMEM)
    hbm = pl.BlockSpec(memory_space=pltpu.HBM)

    got_one, got_two = move(view_one, SWAP), move(view_two, SWAP)
    keep, pull, place = pl.pallas_call(
        functools.partial(choose_kernel, inv_weight / (batch_rows * feature_count)),
        in_specs=[smem, smem, vmem, vmem],
        out_specs=[vmem, vmem, smem],
        out_shape=[
            jax.ShapeDtypeStruct(view_one.shape, jnp.bfloat16),
            jax.ShapeDtypeStruct((shard_rows, width), jnp.float32),
            jax.ShapeDtypeStruct((1,), jnp.int32),
        ],
        compiler_params=room(4),
        name="choose_view",
    )(core, place, *[pltpu.with_memory_space_constraint(v, pltpu.HBM) for v in (view_one, view_two)])
    blocks = pl.pallas_call(
        pack_kernel,
        in_specs=[smem, vmem, vmem, vmem],
        out_specs=vmem,
        out_shape=jax.ShapeDtypeStruct((feature_parts, rows, width), jnp.bfloat16),
        compiler_params=room(4),
        name="pack_rows",
    )(core, keep, got_one, got_two)
    own = exchange(blocks)
    half = width // 2
    halves = own[:, :, :half], own[:, :, half:]
    copies = [[move(h, pairs) for pairs in (FAR, UP, DOWN)] for h in halves]
    (far, up, down), (far_second, up_second, down_second) = copies
    rounded_shape = jax.ShapeDtypeStruct((batch_rows, half), jnp.bfloat16)
    stats_shape = jax.ShapeDtypeStruct((4, half), jnp.float32)
    first, first_stats = pl.pallas_call(
        functools.partial(center_kernel, sizes),
        in_specs=[vmem] * 5,
        out_specs=[vmem] * 2,
        out_shape=[rounded_shape, stats_shape],
        compiler_params=room(12),
        name="center_first",
    )(pull[:, :half], halves[0], up, down, far)
    second, part, second_stats = pl.pallas_call(
        functools.partial(gram_kernel, sizes),
        in_specs=[vmem] * 6,
        out_specs=[vmem] * 3,
        out_shape=[
            rounded_shape,
            jax.ShapeDtypeStruct((feature_parts, rows, batch_rows), jnp.bfloat16),
            stats_shape,
        ],
        compiler_params=room(16),
        name="gram_part",
    )(pull[:, half:], halves[1], up_second, down_second, far_second, first)

    pieces = exchange(part)
    sent = pl.pallas_call(
        functools.partial(sum_kernel, sizes),
        in_specs=[smem, vmem, vmem, vmem],
        out_specs=vmem,
        out_shape=jax.ShapeDtypeStruct((feature_parts, rows, batch_rows), jnp.bfloat16),
        compiler_params=room(4),
        name="gram_sum",
    )(place, pieces, first_stats, second_stats)

    gram = exchange(sent)
    grads, scalar = pl.pallas_call(
        functools.partial(grad_kernel, sizes),
        in_specs=[vmem] * 6,
        out_specs=[hbm, vmem],
        out_shape=[
            pltpu.HBM((feature_parts, rows, width), jnp.bfloat16),
            jax.ShapeDtypeStruct((8, LANES), jnp.float32),
        ],
        scratch_shapes=[
            pltpu.VMEM((group_rows, group_rows), jnp.bfloat16),
            pltpu.VMEM((2, feature_parts, rows, half), jnp.bfloat16),
            pltpu.SemaphoreType.DMA((2,)),
        ],
        compiler_params=room(16),
        name="grad_rows",
    )(gram, first, second, own, first_stats, second_stats)

    grads = exchange(grads)
    far, before, after = [move(scalar, pairs) for pairs in (FAR, UP, DOWN)]
    scalar = (scalar + far) + (before + after)
    other_scalar = move(scalar, SWAP)
    cut, scalar, other_scalar = lax.optimization_barrier(
        (grads[:, shard_rows:], scalar, other_scalar)
    )
    others = move(cut, SWAP)
    grad_one, grad_two, loss = pl.pallas_call(
        final_kernel,
        in_specs=[smem] + [vmem] * 6,
        out_specs=[vmem, vmem, smem],
        out_shape=[
            jax.ShapeDtypeStruct(view_one.shape, jnp.float32),
            jax.ShapeDtypeStruct(view_one.shape, jnp.float32),
            jax.ShapeDtypeStruct((1,), jnp.float32),
        ],
        compiler_params=room(4),
        name="add_pull",
    )(core, grads, others, scalar, other_scalar, view_one, view_two)
    return grad_one, grad_two, loss.reshape(())


def solution(mesh):
    fine = Mesh(np.asarray(mesh.devices).reshape(SIZES), FINE)
    rows = P(FINE, None)
    return jax.shard_map(
        body, mesh=fine, in_specs=(rows, rows), out_specs=(rows, rows, P()), check_vma=False
    )
```

```python
import functools

import jax
import jax.numpy as jnp
import numpy as np
from jax import lax
from jax.experimental import pallas as pl
from jax.experimental.pallas import tpu as pltpu
from jax.sharding import Mesh
from jax.sharding import PartitionSpec as P

epsilon = 0.0001
inv_weight = 25.0
var_weight = 25.0
cov_weight = 1.0
out_scale = 25.0

FINE = ("zh", "x", "y", "zl", "core")
SIZES = (2, 4, 4, 2, 2)
LANES = 128
CHUNK = 512
CONTRACT_LAST = (((1,), (1,)), ((), ()))
CONTRACT_FIRST = (((1,), (0,)), ((), ()))

IDS = np.arange(128).reshape(SIZES)
BY_RING = np.stack(
    [
        IDS[..., 0].transpose(1, 0, 2, 3).reshape(4, 16),
        IDS[..., 1].transpose(2, 0, 1, 3).reshape(4, 16),
    ]
)
GROUPS = [[int(i) for i in g] for core in BY_RING for g in core]
SWAP = [(int(i), int(i) ^ 1) for i in IDS.reshape(-1)]


def along_ring(source):
    return [
        (int(BY_RING[k, source[i], c]), int(BY_RING[k, i, c]))
        for k in range(2)
        for i in range(4)
        for c in range(16)
    ]


UP = along_ring((3, 0, 1, 2))
DOWN = along_ring((1, 2, 3, 0))
FAR = along_ring((2, 3, 0, 1))


def exchange(blocks):
    return lax.all_to_all(blocks, FINE, 0, 0, tiled=True, axis_index_groups=GROUPS)


def move(block, pairs):
    return lax.ppermute(block, FINE, pairs)


def room(mebibytes):
    return pltpu.CompilerParams(vmem_limit_bytes=mebibytes * 1024 * 1024)


def pick(core, first, second):
    return jnp.where(core == 0, first, second)


def choose_kernel(factor, core, place_in, view_one, view_two, keep, squares, place):
    place[0] = place_in[0]
    width = squares.shape[1]
    total = 0.0
    for start in range(0, keep.shape[1], width):
        cut = pl.ds(start, width)
        first = view_one[:, cut].astype(jnp.float32)
        second = view_two[:, cut].astype(jnp.float32)
        keep[:, cut] = pick(core[0], first, second).astype(jnp.bfloat16)
        total += (first - second) ** 2
    squares[...] = factor * total


def pack_kernel(core, keep, got_one, got_two, packed):
    parts, rows, width = packed.shape
    for c in range(parts):
        cut = pl.ds(c * width, width)
        mine, first, second = [ref[:, cut].astype(jnp.float32) for ref in (keep, got_one, got_two)]
        more = pick(core[0], first, second)
        packed[c] = jnp.concatenate([mine, more], axis=0).astype(jnp.bfloat16)


def folded(block):
    return jnp.sum(block.reshape(-1, 8, block.shape[1]), axis=0)


def center_kernel(sizes, pull, own, up, down, far, rounded, stats):
    copies = (up, down, far)
    batch_rows, feature_count, row_parts = sizes
    width = own.shape[2]
    for start in range(0, width, CHUNK):
        cut = pl.ds(start, CHUNK)
        blocks = [(ref, c) for ref in (own,) + copies for c in range(ref.shape[0])]
        total = 0.0
        for ref, c in blocks:
            total += folded(ref[c, :, cut].astype(jnp.float32))
        mean = jnp.sum(total, axis=0, keepdims=True) / batch_rows
        square, energy = 0.0, 0.0
        for i, (ref, c) in enumerate(blocks):
            a = ref[c, :, cut].astype(jnp.float32) - mean
            square += folded(a * a)
            a = a.astype(jnp.bfloat16)
            rounded[pl.ds(i * a.shape[0], a.shape[0]), cut] = a
            a = a.astype(jnp.float32)
            energy += folded(a * a)
        square = jnp.sum(square, axis=0, keepdims=True)
        energy = jnp.sum(energy, axis=0, keepdims=True)
        spread = jnp.sqrt(square / (batch_rows - 1) + epsilon)
        share = var_weight / feature_count / row_parts * jnp.maximum(1.0 - spread, 0.0)
        share -= cov_weight / feature_count / row_parts * (energy / (batch_rows - 1)) ** 2
        share += jnp.sum(pull[:, cut], axis=0, keepdims=True)
        stats[0:1, cut] = mean
        stats[1:2, cut] = energy
        stats[2:3, cut] = jnp.where(spread < 1.0, 1.0 / spread, 0.0)
        stats[3:4, cut] = share


def first_kernel(sizes, pull, own, up, down, far, rounded, stats, product):
    center_kernel(sizes, pull, own, up, down, far, rounded, stats)
    mine = rounded[pl.ds(0, product.shape[0])]
    product[...] = lax.dot_general(
        mine, rounded[...], CONTRACT_LAST, preferred_element_type=jnp.float32
    )


def gram_kernel(sizes, pull, own, up, down, far, partial, second, part, stats):
    batch_rows, feature_count, row_parts = sizes
    group_rows = batch_rows // row_parts
    center_kernel(sizes, pull, own, up, down, far, second, stats)
    product = partial[...] + lax.dot_general(
        second[pl.ds(0, group_rows)], second[...], CONTRACT_LAST, preferred_element_type=jnp.float32
    )
    part[...] = product.astype(jnp.bfloat16).reshape(part.shape)


def slots(shape, rows, first, shift):
    row = lax.broadcasted_iota(jnp.int32, shape, 0)
    lane = lax.broadcasted_iota(jnp.int32, shape, 1)
    inside = row % rows
    return lane == first + row - inside + (inside + shift) % rows


def three_parts(value, shape):
    value = jnp.full(shape, value, jnp.float32)
    high = value.astype(jnp.bfloat16).astype(jnp.float32)
    middle = (value - high).astype(jnp.bfloat16).astype(jnp.float32)
    row = lax.broadcasted_iota(jnp.int32, shape, 0)
    low = jnp.where(row == 2, value - high - middle, 0.0)
    return jnp.where(row == 0, high, jnp.where(row == 1, middle, low))


def sum_kernel(sizes, place, pieces, first_stats, second_stats, sent):
    batch_rows, feature_count, row_parts = sizes
    rows = pieces.shape[1]
    summed = jnp.sum(pieces[...].astype(jnp.float32), axis=0)
    shape = summed.shape
    first = place[0] * rows
    short = summed.astype(jnp.bfloat16).astype(jnp.float32)
    diagonal = slots(shape, rows, first, 0)
    lost = jnp.sum(jnp.where(diagonal, summed - short, 0.0), axis=1, keepdims=True)
    factor = cov_weight / feature_count / (batch_rows - 1) ** 2
    shares = jnp.concatenate([first_stats[3:4], second_stats[3:4]], axis=1)
    value = jnp.sum(factor * jnp.sum(summed * summed, axis=0, keepdims=True) + shares)
    out = jnp.where(slots(shape, rows, first, rows - 1), lost, short)
    out = jnp.where(slots(shape, rows, first, rows - 2), three_parts(value, (rows, 1)), out)
    sent[...] = jnp.broadcast_to(out.astype(jnp.bfloat16)[None], sent.shape)


def grad_kernel(
    sizes, gram, first, second, own, first_stats, second_stats, sent, scalar, left, ready, sems
):
    batch_rows, feature_count, row_parts = sizes
    parts, rows, width = own.shape
    group_rows = parts * rows
    factor_cov = 4.0 * cov_weight * batch_rows / (batch_rows - 1) ** 2 / out_scale
    factor_var = var_weight * batch_rows / (batch_rows - 1) / out_scale

    left[...] = gram[:, :, pl.ds(0, group_rows)].reshape(left.shape)
    shape = (LANES, LANES)
    lane = lax.broadcasted_iota(jnp.int32, (1, LANES), 1) % rows
    lost, shares = [], 0.0
    for start in range(0, group_rows, LANES):
        square = left[pl.ds(start, LANES), pl.ds(start, LANES)].astype(jnp.float32)
        restored = square
        for shift in (1, 2):
            mirror = jnp.where(slots(shape, rows, 0, shift), square, 0.0)
            mirror = jnp.sum(mirror, axis=0, keepdims=True)
            ahead = pltpu.roll(mirror, LANES - shift, 1)
            around = pltpu.roll(mirror, rows - shift, 1)
            mirror = jnp.where(lane < rows - shift, ahead, around)
            here = slots(shape, rows, 0, rows - shift)
            restored = jnp.where(here, mirror, restored)
            taken = jnp.where(here, square, 0.0)
            if shift == 1:
                lost.append(jnp.sum(taken, axis=1, keepdims=True))
            else:
                shares += jnp.sum(taken, axis=0, keepdims=True)
        left[pl.ds(start, LANES), pl.ds(start, LANES)] = restored.astype(jnp.bfloat16)
    lost = jnp.concatenate(lost, axis=0)
    scalar[...] = jnp.full(scalar.shape, jnp.sum(shares), jnp.float32)
    right = gram[:, :, pl.ds(group_rows, batch_rows - group_rows)]
    right = right.reshape(group_rows, batch_rows - group_rows)
    copies = []
    half = width // 2
    for i, (rounded, stats) in enumerate(((first, first_stats), (second, second_stats))):
        cut = pl.ds(i * half, half)
        product = lax.dot_general(
            left[...], rounded[pl.ds(0, group_rows)], CONTRACT_FIRST, preferred_element_type=jnp.float32
        )
        product += lax.dot_general(
            right,
            rounded[pl.ds(group_rows, batch_rows - group_rows)],
            CONTRACT_FIRST,
            preferred_element_type=jnp.float32,
        )
        mine = rounded[pl.ds(0, group_rows)].astype(jnp.float32)
        centered = own[:, :, cut].reshape(group_rows, half).astype(jnp.float32) - stats[0:1]
        product = product + (lost - stats[1:2]) * mine
        grad = factor_cov * product - factor_var * stats[2:3] * centered
        ready[i] = grad.astype(jnp.bfloat16).reshape(parts, rows, half)
        copies.append(pltpu.make_async_copy(ready.at[i], sent.at[:, :, cut], sems.at[i]))
        copies[-1].start()
    for copy in copies:
        copy.wait()


def final_kernel(core, recv, got, mine, other, view_one, view_two, grad_one, grad_two, loss):
    parts, rows, width = got.shape
    push = 2.0 * inv_weight / out_scale
    for c in range(parts):
        own_rows = recv[c].astype(jnp.float32)[:rows]
        more = got[c].astype(jnp.float32)
        cut = pl.ds(c * width, width)
        diff = push * (view_one[:, cut].astype(jnp.float32) - view_two[:, cut].astype(jnp.float32))
        grad_one[:, cut] = pick(core[0], own_rows, more) + diff
        grad_two[:, cut] = pick(core[0], more, own_rows) - diff
    loss[0] = jnp.max(mine[...] + other[...])


def body(view_one, view_two):
    shard_rows, feature_count = view_one.shape
    row_parts, feature_parts = BY_RING.shape[1:]
    batch_rows = shard_rows * 2 * row_parts * feature_parts
    group_rows = batch_rows // row_parts
    width = feature_count // feature_parts
    rows = 2 * shard_rows
    sizes = (batch_rows, feature_count, row_parts)
    core = lax.axis_index("core")
    across = pick(core, lax.axis_index("y"), lax.axis_index("x"))
    place = (lax.axis_index("zh") * 4 + across) * 2 + lax.axis_index("zl")
    core = core.astype(jnp.int32).reshape(1)
    place = place.astype(jnp.int32).reshape(1)
    smem = pl.BlockSpec(memory_space=pltpu.SMEM)
    vmem = pl.BlockSpec(memory_space=pltpu.VMEM)
    hbm = pl.BlockSpec(memory_space=pltpu.HBM)

    got_one, got_two = move(view_one, SWAP), move(view_two, SWAP)
    keep, pull, place = pl.pallas_call(
        functools.partial(choose_kernel, inv_weight / (batch_rows * feature_count)),
        in_specs=[smem, smem, vmem, vmem],
        out_specs=[vmem, vmem, smem],
        out_shape=[
            jax.ShapeDtypeStruct(view_one.shape, jnp.bfloat16),
            jax.ShapeDtypeStruct((shard_rows, width), jnp.float32),
            jax.ShapeDtypeStruct((1,), jnp.int32),
        ],
        compiler_params=room(4),
        name="choose_view",
    )(core, place, *[pltpu.with_memory_space_constraint(v, pltpu.HBM) for v in (view_one, view_two)])
    blocks = pl.pallas_call(
        pack_kernel,
        in_specs=[smem, vmem, vmem, vmem],
        out_specs=vmem,
        out_shape=jax.ShapeDtypeStruct((feature_parts, rows, width), jnp.bfloat16),
        compiler_params=room(4),
        name="pack_rows",
    )(core, keep, got_one, got_two)
    own = exchange(blocks)
    half = width // 2
    halves = own[:, :, :half], own[:, :, half:]
    copies = [[move(h, pairs) for pairs in (FAR, UP, DOWN)] for h in halves]
    (far, up, down), (far_second, up_second, down_second) = copies
    rounded_shape = jax.ShapeDtypeStruct((batch_rows, half), jnp.bfloat16)
    stats_shape = jax.ShapeDtypeStruct((4, half), jnp.float32)
    first, first_stats, partial = pl.pallas_call(
        functools.partial(first_kernel, sizes),
        in_specs=[vmem] * 5,
        out_specs=[vmem] * 3,
        out_shape=[
            rounded_shape,
            stats_shape,
            jax.ShapeDtypeStruct((batch_rows // row_parts, batch_rows), jnp.float32),
        ],
        compiler_params=room(12),
        name="center_first",
    )(pull[:, :half], halves[0], up, down, far)
    second, part, second_stats = pl.pallas_call(
        functools.partial(gram_kernel, sizes),
        in_specs=[vmem] * 6,
        out_specs=[vmem] * 3,
        out_shape=[
            rounded_shape,
            jax.ShapeDtypeStruct((feature_parts, rows, batch_rows), jnp.bfloat16),
            stats_shape,
        ],
        compiler_params=room(16),
        name="gram_part",
    )(pull[:, half:], halves[1], up_second, down_second, far_second, partial)

    pieces = exchange(part)
    sent = pl.pallas_call(
        functools.partial(sum_kernel, sizes),
        in_specs=[smem, vmem, vmem, vmem],
        out_specs=vmem,
        out_shape=jax.ShapeDtypeStruct((feature_parts, rows, batch_rows), jnp.bfloat16),
        compiler_params=room(4),
        name="gram_sum",
    )(place, pieces, first_stats, second_stats)

    gram = exchange(sent)
    grads, scalar = pl.pallas_call(
        functools.partial(grad_kernel, sizes),
        in_specs=[vmem] * 6,
        out_specs=[hbm, vmem],
        out_shape=[
            pltpu.HBM((feature_parts, rows, width), jnp.bfloat16),
            jax.ShapeDtypeStruct((8, LANES), jnp.float32),
        ],
        scratch_shapes=[
            pltpu.VMEM((group_rows, group_rows), jnp.bfloat16),
            pltpu.VMEM((2, feature_parts, rows, half), jnp.bfloat16),
            pltpu.SemaphoreType.DMA((2,)),
        ],
        compiler_params=room(16),
        name="grad_rows",
    )(gram, first, second, own, first_stats, second_stats)

    grads = exchange(grads)
    far, before, after = [move(scalar, pairs) for pairs in (FAR, UP, DOWN)]
    scalar = (scalar + far) + (before + after)
    cut, scalar = lax.optimization_barrier((grads[:, shard_rows:], scalar))
    others, other_scalar = move(cut, SWAP), move(scalar, SWAP)
    grad_one, grad_two, loss = pl.pallas_call(
        final_kernel,
        in_specs=[smem] + [vmem] * 6,
        out_specs=[vmem, vmem, smem],
        out_shape=[
            jax.ShapeDtypeStruct(view_one.shape, jnp.float32),
            jax.ShapeDtypeStruct(view_one.shape, jnp.float32),
            jax.ShapeDtypeStruct((1,), jnp.float32),
        ],
        compiler_params=room(4),
        name="add_pull",
    )(core, grads, others, scalar, other_scalar, view_one, view_two)
    return grad_one, grad_two, loss.reshape(())


def solution(mesh):
    fine = Mesh(np.asarray(mesh.devices).reshape(SIZES), FINE)
    rows = P(FINE, None)
    return jax.shard_map(
        body, mesh=fine, in_specs=(rows, rows), out_specs=(rows, rows, P()), check_vma=False
    )
```
